32 devices in a mesh: ctx: 8 (over z, y), fsdp: 4 (over x, core).
Axes of the slice: x: 2, y: 2, z: 4, core: 2. Of those that a mesh axis runs over, the one named last changes fastest.
Arguments:
- hidden_in: bfloat16 [8, 8, 256, 576], P('fsdp', 'ctx'), may hold values from -6 to 6
- cotangent: bfloat16 [8, 8, 256, 576], P('fsdp', 'ctx'), may hold values from -6 to 6
- span_table: int32 [8], replicated, may hold values from 0 to 7, as said below
- positions: int32 [8, 8, 256], P('fsdp', 'ctx'), may hold values from 0 to 4095, as said below
- attn_gain: bfloat16 [576], P('fsdp'), may hold values from 0.5 to 1.5
- w_query: bfloat16 [576, 576], P('fsdp'), may hold values from -0.25 to 0.25
- w_key: bfloat16 [576, 192], P('fsdp'), may hold values from -0.25 to 0.25
- w_value: bfloat16 [576, 192], P('fsdp'), may hold values from -0.25 to 0.25
- w_out: bfloat16 [576, 576], P('fsdp'), may hold values from -3 to 3
- ffn_gain: bfloat16 [576], P('fsdp'), may hold values from 0.5 to 1.5
- w_gate: bfloat16 [576, 1536], P('fsdp'), may hold values from -0.25 to 0.25
- w_up: bfloat16 [576, 1536], P('fsdp'), may hold values from -0.25 to 0.25
- w_down: bfloat16 [1536, 576], P('fsdp'), may hold values from -0.15625 to 0.15625
Outputs:
- hidden_out: bfloat16 [8, 8, 256, 576], P('fsdp', 'ctx')
- grad_input: float32 [8, 8, 256, 576], P('fsdp', 'ctx')
- grad_query: float32 [576, 576], P('fsdp')
- grad_key: float32 [576, 192], P('fsdp')
- grad_value: float32 [576, 192], P('fsdp')
- grad_out: float32 [576, 576], P('fsdp')
- grad_gate: float32 [576, 1536], P('fsdp')
- grad_up: float32 [576, 1536], P('fsdp')
- grad_down: float32 [1536, 576], P('fsdp')
- grad_attn_gain: float32 [576], P('fsdp')
- grad_ffn_gain: float32 [576], P('fsdp')
The draws below stay inside these ranges and needn't reach their ends.
Inputs may be any that keep to these rules, and one draw needn't show every extreme that they name: `span_table`: a permutation of 0 to 7. `positions`: a token's position is its place in the sequence (by span_table) plus a start of its own sequence; the starts lie in 0 to 2048.
All inputs are finite; a program needn't handle non-finite values.
Results may differ from the reference program's by a relative error of at most 0.017.
Values may be sent and summed in bfloat16 or wider, within the bound.
A program may use at most 128 MiB of HBM per device.

```python
import math
import jax
import jax.numpy as jnp
from jax import lax

D = 576
HQ = 9
HK = 3
HD = 64
FF = 1536
SPAN = 128
SEQ_LEN = 2048
NSEQ = 8
N_CTX = 8


def pair_table(key):
    return jax.random.permutation(key, N_CTX).astype(jnp.int32)


def draw_span_table(key, part):
    return pair_table(key)


def draw_positions(key, part):
    table = pair_table(key)
    key = jax.random.fold_in(key, 5)
    start_key, pick_key = jax.random.split(key)
    starts = jax.random.randint(start_key, (NSEQ,), 0, SEQ_LEN + 1).astype(jnp.int32)
    picked = jax.random.permutation(pick_key, NSEQ).astype(jnp.int32)
    starts = starts.at[picked[0]].set(0).at[picked[1]].set(SEQ_LEN)
    columns = jnp.arange(2 * SPAN, dtype=jnp.int32)
    span_ids = jnp.where(columns[None, :] < SPAN, table[:, None], 2 * N_CTX - 1 - table[:, None])
    order = span_ids * SPAN + columns[None, :] % SPAN
    return (starts[:, None, None] + order[None, :, :]).astype(jnp.int32)


def steps_of(key, shape, shards, least, high):
    loudness, own = 1.0, jax.random.fold_in(key, 6)
    for position, shards_of in shards:
        draws = jnp.exp(jax.random.uniform(jax.random.fold_in(own, position), (shards_of,), jnp.float32, least / len(shards), high / len(shards)))
        loudness = loudness * jnp.repeat(draws, shape[position] // shards_of).reshape([-1 if axis == position else 1 for axis in range(len(shape))])
    return loudness


def noise(stream_key, extent, width, most, pieces=(), kind=jnp.bfloat16):
    drawn = width * jax.random.normal(stream_key, extent, jnp.float32)
    if pieces:
        drawn = drawn * steps_of(stream_key, extent, pieces, -0.22, 0.18)
    return jnp.clip(drawn, -most, most).astype(kind)


def setup_inputs(seed: int = 0) -> dict:
    key_of = jax.random.split(jax.random.key(seed), 14)
    return {
        "hidden_in": noise(key_of[0], (NSEQ, N_CTX, 2 * SPAN, D), 1.0, 6.0, ((0, 4), (1, 8))),
        "cotangent": noise(key_of[1], (NSEQ, N_CTX, 2 * SPAN, D), 1.0, 6.0, ((0, 4), (1, 8))),
        "span_table": draw_span_table(jax.random.fold_in(key_of[13], 71), 0),
        "positions": draw_positions(jax.random.fold_in(key_of[13], 71), 0),
        "attn_gain": jnp.clip(1.0 + 0.1 * jax.random.normal(key_of[4], (D,), jnp.float32), 0.5, 1.5).astype(jnp.bfloat16),
        "w_query": noise(key_of[5], (D, HQ * HD), D ** -0.5, 0.25, ((0, 4),)),
        "w_key": noise(key_of[6], (D, HK * HD), D ** -0.5, 0.25, ((0, 4),)),
        "w_value": noise(key_of[7], (D, HK * HD), D ** -0.5, 0.25, ((0, 4),)),
        "w_out": noise(key_of[8], (HQ * HD, D), (max(1, HQ * HD * 16 // SEQ_LEN)) ** -0.5, 3.0, ((0, 4),)),
        "ffn_gain": jnp.clip(1.0 + 0.1 * jax.random.normal(key_of[9], (D,), jnp.float32), 0.5, 1.5).astype(jnp.bfloat16),
        "w_gate": noise(key_of[10], (D, FF), D ** -0.5, 0.25, ((0, 4),)),
        "w_up": noise(key_of[11], (D, FF), D ** -0.5, 0.25, ((0, 4),)),
        "w_down": noise(key_of[12], (FF, D), FF ** -0.5, 0.15625, ((0, 4),)),
    }


EPS = 1e-05
THETA = 100000.0

@jax.custom_vjp
def low(v):
    return lax.optimization_barrier(v.astype(jnp.bfloat16)).astype(jnp.float32)

@jax.custom_vjp
def low_back(v):
    return v

def low_keep(v):
    return (low(v), None)

def low_pass(kept, grad):
    return (grad,)

def back_keep(v):
    return (v, None)

def back_low(kept, grad):
    return (low(grad),)
low.defvjp(low_keep, low_pass)
low_back.defvjp(back_keep, back_low)

def rotate(vector, cosine, sine):
    half_dim = vector.shape[-1] // 2
    first = vector[..., :half_dim]
    second = vector[..., half_dim:]
    return jnp.concatenate([first * cosine - second * sine, second * cosine + first * sine], axis=-1)

def rope_tables(place, head_dim):
    half_dim = head_dim // 2
    inverse = jnp.exp(jnp.arange(half_dim, dtype=jnp.float32) * (-math.log(THETA) / half_dim))
    angles = place.astype(jnp.float32)[:, None] * inverse[None, :]
    return (jnp.cos(angles)[:, None, :], jnp.sin(angles)[:, None, :])

def normed(vector, gain_vec):
    return vector * lax.rsqrt(lax.optimization_barrier(jnp.mean(vector * vector, axis=-1, keepdims=True)) + EPS) * gain_vec

def matmul(left, right):
    return jnp.dot(left, right, precision=lax.Precision.HIGHEST)

def attend_block(query_blk, order_blk, key_rows, value_rows, key_order):
    scores = jnp.einsum('qgrd,kgd->grqk', query_blk, key_rows, precision=lax.Precision.HIGHEST) * (1.0 / math.sqrt(HD))
    scores = low_back(scores)
    scores = jnp.where(key_order[None, None, None, :] <= order_blk[None, None, :, None], scores, -1e+30)
    probs = low(jax.nn.softmax(scores, axis=-1))
    return jnp.einsum('grqk,kgd->qgrd', probs, value_rows, precision=lax.Precision.HIGHEST)

def layer_sequence(seq_rows, seq_place, key_order, weights):
    w_query, w_key, w_value, w_out, w_gate, w_up, w_down, gain_one, gain_two = weights
    length = seq_rows.shape[0]
    cosine, sine = rope_tables(seq_place, HD)
    first_in = low(normed(seq_rows, gain_one))
    query_rows = low(rotate(low_back(matmul(first_in, w_query)).reshape(length, HQ, HD), cosine, sine))
    key_rows = low(rotate(low_back(matmul(first_in, w_key)).reshape(length, HK, HD), cosine, sine))
    value_rows = low(low_back(matmul(first_in, w_value))).reshape(length, HK, HD)
    block_rows = min(512, length)
    query_blocks = query_rows.reshape(length // block_rows, block_rows, HK, HQ // HK, HD)
    order_blocks = key_order.reshape(length // block_rows, block_rows)
    stepper = jax.checkpoint(attend_block)
    attended = lax.map(lambda inputs: stepper(inputs[0], inputs[1], key_rows, value_rows, key_order), (query_blocks, order_blocks))
    attended = low(low_back(attended.reshape(length, HQ * HD)))
    middle = seq_rows + low_back(matmul(attended, w_out))
    second_in = low(normed(middle, gain_two))
    gate_proj = low_back(matmul(second_in, w_gate))
    up_proj = low_back(matmul(second_in, w_up))
    hidden = low(jax.nn.silu(gate_proj) * up_proj)
    return middle + low_back(matmul(hidden, w_down))

def reference(hidden_in, cotangent, span_table, positions, attn_gain, w_query, w_key, w_value, w_out, ffn_gain, w_gate, w_up, w_down):
    weights = tuple((item.astype(jnp.float32) for item in (w_query, w_key, w_value, w_out, w_gate, w_up, w_down, attn_gain, ffn_gain)))
    seq_rows = hidden_in.astype(jnp.float32).reshape(NSEQ, SEQ_LEN, D)
    places = positions.reshape(NSEQ, SEQ_LEN)
    columns = jnp.arange(2 * SPAN, dtype=jnp.int32)
    span_ids = jnp.where(columns[None, :] < SPAN, span_table[:, None], 2 * N_CTX - 1 - span_table[:, None])
    key_order = (span_ids * SPAN + columns[None, :] % SPAN).astype(jnp.int32).reshape(SEQ_LEN)

    def forward(rows_all, *weight_list):
        return lax.map(lambda inputs: layer_sequence(inputs[0], inputs[1], key_order, weight_list), (rows_all, places))
    output, pullback = jax.vjp(forward, seq_rows, *weights)
    grads = pullback(cotangent.astype(jnp.float32).reshape(NSEQ, SEQ_LEN, D))
    return (output.astype(jnp.bfloat16).reshape(hidden_in.shape), grads[0].reshape(hidden_in.shape), grads[1], grads[2], grads[3], grads[4], grads[5], grads[6], grads[7], grads[8], grads[9])
```

```python
import functools
import math

import jax
import jax.numpy as jnp
from jax import lax
from jax.experimental import pallas as pl
from jax.experimental.pallas import tpu as pltpu
from jax.sharding import PartitionSpec as P

HQ = 9
HK = 3
HD = 64


EPS = 1e-05
THETA = 100000.0


def rotate(vector, cosine, sine):
    half_dim = vector.shape[-1] // 2
    first = vector[..., :half_dim]
    second = vector[..., half_dim:]
    return jnp.concatenate(
        [first * cosine - second * sine, second * cosine + first * sine], axis=-1
    )


def rope_tables(place, head_dim):
    half_dim = head_dim // 2
    inverse = jnp.exp(jnp.arange(half_dim, dtype=jnp.float32) * (-math.log(THETA) / half_dim))
    angles = place.astype(jnp.float32)[:, None] * inverse[None, :]
    return (jnp.cos(angles)[:, None, :], jnp.sin(angles)[:, None, :])


def norm_back(vector, inverse, gain_vec, incoming):
    scaled = incoming * gain_vec
    gain_grad = jnp.sum(incoming * vector * inverse, axis=0)
    vector_grad = inverse * scaled - vector * (inverse * inverse * inverse) * jnp.mean(
        scaled * vector, axis=-1, keepdims=True
    )
    return (vector_grad, gain_grad)


MESH = pl.DeviceIdType.MESH
VMEM = pltpu.VMEM
BIG = 56 * 1024 * 1024


def ring_pos(index, count):
    odd = lax.rem(index, 2)
    return (1 - odd) * (index // 2) + odd * (count - 1 - index // 2)


def ring_index(place, count):
    place = lax.rem(place + 2 * count, count)
    back = place // (count // 2)
    return (1 - back) * (2 * place) + back * (2 * (count - 1 - place) + 1)


def neighbours(count):
    me = lax.axis_index("ctx")
    shard = lax.axis_index("fsdp")
    place = ring_pos(me, count)
    core = shard + 1 - 2 * lax.rem(shard, 2)
    across = lax.rem(shard + 2, 4)
    right = (ring_index(place + 1, count), shard)
    left = (ring_index(place - 1, count), shard)
    return me, shard, place, (me, core), (me, across), right, left


def greet(partners):
    barrier = pltpu.get_barrier_semaphore()
    for partner in partners:
        pl.semaphore_signal(barrier, inc=1, device_id=partner, device_id_type=MESH)
    pl.semaphore_wait(barrier, len(partners))


def remote(source, target, send, recv, device):
    return pltpu.make_async_remote_copy(
        src_ref=source,
        dst_ref=target,
        send_sem=send,
        recv_sem=recv,
        device_id=device,
        device_id_type=MESH,
    )


def comm_call(kernel, out_shape, scratch, cid, args):
    vm = pl.BlockSpec(memory_space=VMEM)
    return pl.pallas_call(
        kernel,
        out_shape=out_shape,
        in_specs=[vm] * len(args),
        out_specs=[vm] * len(out_shape),
        scratch_shapes=scratch,
        compiler_params=pltpu.CompilerParams(
            collective_id=cid, has_side_effects=True, vmem_limit_bytes=BIG
        ),
    )(*args)


class WeightGather:
    def __init__(self, ins, outs, sems, base, shard, core, across):
        self.parts = []
        for k, (src, dst) in enumerate(zip(ins, outs)):
            rows = src.shape[0]

            def slot(owner, dst=dst, rows=rows):
                return dst.at[pl.ds(pl.multiple_of(owner * rows, 16), rows)]

            other_core = shard + 1 - 2 * lax.rem(shard, 2)
            over = lax.rem(shard + 2, 4)
            sem = lambda j, k=k: (sems.at[0, base + k, j], sems.at[1, base + k, j])
            cross = remote(src, slot(shard), *sem(0), across)
            near = remote(src, slot(shard), *sem(1), core)
            onward = remote(slot(over), slot(over), *sem(2), core)
            self.parts.append((cross, near, onward, src, dst, shard, rows))

    def start(self):
        for cross, near, *_ in self.parts:
            cross.start()
            near.start()
        for _, _, _, src, dst, shard, rows in self.parts:
            dst[pl.ds(pl.multiple_of(shard * rows, 16), rows)] = src[...]

    def forward(self):
        for cross, _, onward, *_ in self.parts:
            cross.wait_recv()
            onward.start()

    def finish(self):
        for cross, near, onward, *_ in self.parts:
            near.wait_recv()
            onward.wait_recv()
            cross.wait_send()
            near.wait_send()
            onward.wait_send()


def gather_small(count, *refs):
    k = (len(refs) - 1) // 2
    ins, outs, sems = refs[:k], refs[k : 2 * k], refs[-1]
    _, shard, _, core, across, _, _ = neighbours(count)
    greet((core, across))
    work = WeightGather(ins, outs, sems, 0, shard, core, across)
    work.start()
    work.forward()
    work.finish()


def gather_weights(count, arrays, cid):
    outs = [jax.ShapeDtypeStruct((4 * a.shape[0], a.shape[1]), a.dtype) for a in arrays]
    return comm_call(
        functools.partial(gather_small, count),
        outs,
        [pltpu.SemaphoreType.DMA((2, len(arrays), 3))],
        cid,
        arrays,
    )


def gather_both_kernel(count, kv_ref, *refs):
    k = (len(refs) - 3) // 2
    ins, all_ref, outs = refs[:k], refs[k], refs[k + 1 : 2 * k + 1]
    sems, ring = refs[-2:]
    me, shard, place, core, across, right, left = neighbours(count)
    greet((core, across, right, left))
    half = count // 2
    rows = kv_ref.shape[0]

    def step(t, way):
        block = ring_index(place - way * (t - 1), count)
        src = kv_ref if t == 1 else all_ref.at[block]
        dst = all_ref.at[block]
        if t == half:
            cut = pl.ds(0, rows // 2) if way > 0 else pl.ds(rows // 2, rows // 2)
            src, dst = src.at[cut], dst.at[cut]
        lane = 0 if way > 0 else 1
        return remote(
            src, dst, ring.at[0, lane, t - 1], ring.at[1, lane, t - 1], right if way > 0 else left
        )

    steps = [(step(t, 1), step(t, -1)) for t in range(1, half + 1)]
    steps[0][0].start()
    steps[0][1].start()
    work = WeightGather(ins, outs, sems, 0, shard, core, across)
    work.start()
    all_ref[me] = kv_ref[...]
    for t in range(1, half):
        for way in (0, 1):
            steps[t - 1][way].wait_recv()
            steps[t][way].start()
    work.forward()
    for way in (0, 1):
        steps[half - 1][way].wait_recv()
    for pair in steps:
        pair[0].wait_send()
        pair[1].wait_send()
    work.finish()


def gather_both(count, kv, arrays, cid):
    outs = [jax.ShapeDtypeStruct((count,) + kv.shape, kv.dtype)]
    outs += [jax.ShapeDtypeStruct((4 * a.shape[0], a.shape[1]), a.dtype) for a in arrays]
    return comm_call(
        functools.partial(gather_both_kernel, count),
        outs,
        [
            pltpu.SemaphoreType.DMA((2, len(arrays), 3)),
            pltpu.SemaphoreType.DMA((2, 2, count // 2)),
        ],
        cid,
        [kv] + list(arrays),
    )


def add_rows(rows, block, body):
    def one(i, carry):
        body(pl.ds(pl.multiple_of(i * block, 16), block))
        return carry

    lax.fori_loop(0, rows // block, one, 0)


class ShardSum:
    def __init__(self, pack, out, near_buf, far_buf, sems, chunks, shard, core, across):
        self.pack, self.out, self.near_buf, self.far_buf = pack, out, near_buf, far_buf
        self.size = pack.shape[1] // chunks
        self.chunks = chunks
        self.mine, self.side = lax.rem(shard, 2), shard // 2
        self.near, self.far = [], []
        for c in range(chunks):
            cut = pl.ds(c * self.size, self.size)
            pair = []
            for x in range(2):
                pair.append(
                    remote(
                        pack.at[2 * x + 1 - self.mine, cut],
                        near_buf.at[x, cut],
                        sems.at[0, c, x],
                        sems.at[1, c, x],
                        core,
                    )
                )
            self.near.append(pair)
            self.far.append(
                remote(
                    near_buf.at[1 - self.side, cut],
                    far_buf.at[cut],
                    sems.at[0, c, 2],
                    sems.at[1, c, 2],
                    across,
                )
            )

    def start(self):
        for pair in self.near:
            for copy in pair:
                copy.start()

    def cross(self, c):
        for copy in self.near[c]:
            copy.wait_recv()

        def body(cut):
            for x in (0, 1):
                total = self.pack[2 * x + self.mine, cut].astype(jnp.float32) + self.near_buf[
                    x, cut
                ].astype(jnp.float32)
                self.near_buf[x, cut] = total.astype(jnp.bfloat16)

        base = c * self.size
        add_rows(self.size, 16, lambda cut: body(pl.ds(pl.multiple_of(base + cut.start, 16), cut.size)))
        self.far[c].start()

    def close(self, c):
        self.far[c].wait_recv()
        self.far[c].wait_send()

        def body(cut):
            total = self.near_buf[self.side, cut].astype(jnp.float32) + self.far_buf[cut].astype(
                jnp.float32
            )
            self.out[cut] = total.astype(jnp.bfloat16)

        base = c * self.size
        add_rows(self.size, 16, lambda cut: body(pl.ds(pl.multiple_of(base + cut.start, 16), cut.size)))

    def finish(self):
        for pair in self.near:
            for copy in pair:
                copy.wait_send()


class RingSum:
    def __init__(self, count, term, rows, cuts, send_buf, recv_buf, sems, place, right, left):
        self.count, self.term, self.rows, self.cuts = count, term, rows, cuts
        self.send_buf, self.recv_buf, self.place = send_buf, recv_buf, place
        self.half = count // 2
        self.copies = []
        for t in range(self.half):
            pair = []
            for lane in (0, 1):
                src, dst = send_buf.at[lane, t], recv_buf.at[lane, t]
                if t == 0:
                    src, dst = src.at[cuts[lane]], dst.at[cuts[lane]]
                pair.append(
                    remote(
                        src, dst, sems.at[0, lane, t], sems.at[1, lane, t], left if lane else right
                    )
                )
            self.copies.append(pair)

    def piece(self, t, lane):
        away = self.half - t
        return ring_index(self.place + (away if lane == 0 else -away), self.count)

    def start(self):
        for lane in (0, 1):
            index = self.piece(0, lane)
            cut = self.cuts[lane]
            self.send_buf[(lane, 0) + cut] = self.term(index)[cut]
            self.copies[0][lane].start()

    def step(self, t):
        for lane in (0, 1):
            self.copies[t - 1][lane].wait_recv()
            index = self.piece(t, lane)
            own = self.term(index)
            if t == 1:
                cut, rest = self.cuts[lane], self.cuts[1 - lane]
                self.send_buf[(lane, t) + rest] = own[rest]
                total = own[cut].astype(jnp.float32) + self.recv_buf[(lane, 0) + cut].astype(
                    jnp.float32
                )
                self.send_buf[(lane, t) + cut] = total.astype(jnp.bfloat16)
            else:

                def body(cut):
                    total = own[cut].astype(jnp.float32) + self.recv_buf[lane, t - 1, cut].astype(
                        jnp.float32
                    )
                    self.send_buf[lane, t, cut] = total.astype(jnp.bfloat16)

                add_rows(self.rows, 16, body)
            self.copies[t][lane].start()

    def last(self, store):
        for lane in (0, 1):
            self.copies[self.half - 1][lane].wait_recv()
        own = self.term(ring_index(self.place, self.count))

        def body(cut):
            total = (
                own[cut].astype(jnp.float32)
                + self.recv_buf[0, self.half - 1, cut].astype(jnp.float32)
                + self.recv_buf[1, self.half - 1, cut].astype(jnp.float32)
            )
            store(cut, total)

        add_rows(self.rows, 16, body)

    def finish(self):
        for pair in self.copies:
            for copy in pair:
                copy.wait_send()


def kv_back_kernel(
    count, chunks, dkv, pack, own_ref, sum_ref, near_buf, far_buf, sends, recvs, sems, ring
):
    me, shard, place, core, across, right, left = neighbours(count)
    greet((core, across, right, left))
    half = count // 2
    rows = dkv.shape[1]
    cuts = ((pl.ds(0, rows // 2),), (pl.ds(rows // 2, rows // 2),))
    turn = RingSum(count, lambda i: dkv.at[i], rows, cuts, sends, recvs, ring, place, right, left)
    turn.start()
    shares = ShardSum(pack, sum_ref, near_buf, far_buf, sems, chunks, shard, core, across)
    shares.start()
    for c in range(chunks):
        shares.cross(c)
    for t in range(1, half):
        turn.step(t)

    def store(cut, total):
        own_ref[cut] = total

    for c in range(chunks):
        shares.close(c)
    turn.last(store)
    turn.finish()
    shares.finish()


def kv_back(count, dkv, pack, cid):
    _, rows, width = dkv.shape
    _, prow, pwid = pack.shape
    chunks = 4
    bf16 = jnp.bfloat16
    half = count // 2
    return comm_call(
        functools.partial(kv_back_kernel, count, chunks),
        [
            jax.ShapeDtypeStruct((rows, width), jnp.float32),
            jax.ShapeDtypeStruct((prow, pwid), bf16),
        ],
        [
            VMEM((2, prow, pwid), bf16),
            VMEM((prow, pwid), bf16),
            VMEM((2, half, rows, width), bf16),
            VMEM((2, half, rows, width), bf16),
            pltpu.SemaphoreType.DMA((2, chunks, 3)),
            pltpu.SemaphoreType.DMA((2, 2, half)),
        ],
        cid,
        [dkv, pack],
    )


class RingGather:
    def __init__(self, count, out, rows, cuts, sems, place, right, left):
        half = count // 2
        self.copies = []
        for t in range(half):
            pair = []
            for lane in (0, 1):
                index = ring_index(place - t if lane == 0 else place + t, count)
                cut = (pl.ds(pl.multiple_of(index * rows, 16), rows),)
                if t == half - 1:
                    cut += cuts[lane][1:]
                pair.append(
                    remote(
                        out.at[cut],
                        out.at[cut],
                        sems.at[0, lane, t],
                        sems.at[1, lane, t],
                        left if lane else right,
                    )
                )
            self.copies.append(pair)

    def start(self):
        for copy in self.copies[0]:
            copy.start()

    def step(self, t):
        for lane in (0, 1):
            self.copies[t - 1][lane].wait_recv()
            self.copies[t][lane].start()

    def finish(self):
        for copy in self.copies[-1]:
            copy.wait_recv()
        for pair in self.copies:
            for copy in pair:
                copy.wait_send()


def ring_parts(count, source, out, sends, recvs, sems_sum, sems_all, place, right, left):
    rows, width = source.shape[0] // count, source.shape[1]
    cuts = ((slice(None), pl.ds(0, width // 2)), (slice(None), pl.ds(width // 2, width // 2)))
    term = lambda i: source.at[pl.ds(pl.multiple_of(i * rows, 16), rows)]
    turn = RingSum(count, term, rows, cuts, sends, recvs, sems_sum, place, right, left)
    spread = RingGather(count, out, rows, cuts, sems_all, place, right, left)
    base = ring_index(place, count) * rows

    def store(cut, total):
        out[pl.ds(pl.multiple_of(base + cut.start, 16), cut.size)] = total.astype(jnp.bfloat16)

    return turn, spread, store


def last_sum_kernel(
    count, part, pack, out_f, out_q, near_buf, far_buf, sum_q,
    sf, rf, sq, rq, sems, ra, rb, rc, rd,
):
    me, shard, place, core, across, right, left = neighbours(count)
    greet((core, across, right, left))
    half = count // 2
    shares = ShardSum(pack, sum_q, near_buf, far_buf, sems, 1, shard, core, across)
    shares.start()
    turn_f, spread_f, store_f = ring_parts(
        count, part, out_f, sf, rf, ra, rb, place, right, left
    )
    turn_q, spread_q, store_q = ring_parts(
        count, sum_q, out_q, sq, rq, rc, rd, place, right, left
    )
    turn_f.start()
    shares.cross(0)
    if half > 1:
        turn_f.step(1)
    shares.close(0)
    turn_q.start()
    for t in range(2, half + 1):
        if t < half:
            turn_f.step(t)
        turn_q.step(t - 1)
    turn_f.last(store_f)
    spread_f.start()
    turn_q.last(store_q)
    spread_q.start()
    for t in range(1, half):
        spread_f.step(t)
        spread_q.step(t)
    spread_f.finish()
    spread_q.finish()
    turn_f.finish()
    turn_q.finish()
    shares.finish()


def last_sum(count, part, pack, cid):
    frow, fwid = part.shape
    _, qrow, qwid = pack.shape
    bf16 = jnp.bfloat16
    half = count // 2
    dma = pltpu.SemaphoreType.DMA
    return comm_call(
        functools.partial(last_sum_kernel, count),
        [jax.ShapeDtypeStruct((frow, fwid), bf16), jax.ShapeDtypeStruct((qrow, qwid), bf16)],
        [
            VMEM((2, qrow, qwid), bf16),
            VMEM((qrow, qwid), bf16),
            VMEM((qrow, qwid), bf16),
            VMEM((2, half, frow // count, fwid), bf16),
            VMEM((2, half, frow // count, fwid), bf16),
            VMEM((2, half, qrow // count, qwid), bf16),
            VMEM((2, half, qrow // count, qwid), bf16),
            dma((2, 1, 3)),
            dma((2, 2, half)),
            dma((2, 2, half)),
            dma((2, 2, half)),
            dma((2, 2, half)),
        ],
        cid,
        [part, pack],
    )


def shards(
    hidden_in,
    cotangent,
    span_table,
    positions,
    attn_gain,
    w_query,
    w_key,
    w_value,
    w_out,
    ffn_gain,
    w_gate,
    w_up,
    w_down,
):
    seq_count = hidden_in.shape[0]
    pair_rows = hidden_in.shape[2]
    width = hidden_in.shape[3]
    span_rows = pair_rows // 2
    ctx_count = lax.axis_size("ctx")
    full_len = ctx_count * pair_rows
    row_count = seq_count * pair_rows
    group_size = HQ // HK
    score_scale = 1.0 / math.sqrt(HD)
    f32 = jnp.float32
    bf16 = jnp.bfloat16
    columns = jnp.arange(pair_rows, dtype=jnp.int32)
    span_ids = jnp.where(
        columns[None, :] < span_rows, span_table[:, None], 2 * ctx_count - 1 - span_table[:, None]
    )
    key_order = (span_ids * span_rows + columns[None, :] % span_rows).reshape(full_len)
    own_order = lax.dynamic_slice_in_dim(key_order, lax.axis_index("ctx") * pair_rows, pair_rows)
    allowed = (key_order[None, :] <= own_order[:, None])[None, :, :]
    gains_own = jnp.concatenate(
        [attn_gain[None], ffn_gain[None], jnp.zeros((14,) + attn_gain.shape, bf16)], axis=0
    )
    qkv_all, gains_all = gather_weights(
        ctx_count, [jnp.concatenate([w_query, w_key, w_value], axis=1), gains_own], 0
    )
    gains_all = gains_all.reshape(4, 16, -1)
    gain_first = gains_all[:, 0].reshape(width)
    gain_second = gains_all[:, 1].reshape(width)
    cosine, sine = rope_tables(positions.reshape(row_count), HD)
    x_rows = hidden_in.reshape(row_count, width).astype(f32)
    inverse_one = lax.rsqrt(jnp.mean(x_rows * x_rows, axis=-1, keepdims=True) + EPS)
    first_in = (x_rows * inverse_one * gain_first.astype(f32)).astype(bf16)
    qkv_rows = jnp.dot(first_in, qkv_all, preferred_element_type=f32)
    q_width, k_width = HQ * HD, HK * HD
    query_rows = rotate(
        qkv_rows[:, :q_width].reshape(row_count, HQ, HD), cosine, sine
    ).astype(bf16)
    key_rows = rotate(
        qkv_rows[:, q_width : q_width + k_width].reshape(row_count, HK, HD), cosine, sine
    ).astype(bf16)
    value_rows = qkv_rows[:, q_width + k_width :].astype(bf16)
    all_kv, wo_all, gu_all, wd_all = gather_both(
        ctx_count,
        jnp.concatenate([key_rows.reshape(row_count, k_width), value_rows], axis=1),
        [w_out, jnp.concatenate([w_gate, w_up], axis=1), w_down],
        1,
    )
    kv_seqs = all_kv.reshape(ctx_count, seq_count, pair_rows, 2 * k_width)
    kv_seqs = jnp.swapaxes(kv_seqs, 0, 1).reshape(seq_count, full_len, 2 * k_width)
    all_keys, all_values = kv_seqs[..., :k_width], kv_seqs[..., k_width:]
    query_seqs = query_rows.reshape(seq_count, pair_rows, HK, group_size, HD)

    def forward_group(parts):
        query_grp, key_grp, value_grp = parts
        scores = (
            jnp.einsum("qrd,kd->rqk", query_grp, key_grp, preferred_element_type=f32) * score_scale
        )
        scores = jnp.where(allowed, scores, -1e30)
        row_max = jnp.max(scores, axis=-1, keepdims=True)
        raised = jnp.exp(scores - row_max)
        row_sum = jnp.sum(raised, axis=-1, keepdims=True)
        probs = (raised / row_sum).astype(bf16)
        attended = jnp.einsum("rqk,kd->qrd", probs, value_grp, preferred_element_type=f32)
        return (attended.astype(bf16), (row_max + jnp.log(row_sum))[..., 0])

    def forward_seq(inputs):
        query_blk, key_blk, value_blk = inputs
        key_full = jnp.moveaxis(key_blk.reshape(full_len, HK, HD), 1, 0)
        value_full = jnp.moveaxis(value_blk.reshape(full_len, HK, HD), 1, 0)
        attended, log_sum = lax.map(
            forward_group, (jnp.moveaxis(query_blk, 1, 0), key_full, value_full)
        )
        return (jnp.moveaxis(attended, 0, 1).reshape(pair_rows, HQ * HD), log_sum)

    mixed_seqs, log_sums = lax.map(forward_seq, (query_seqs, all_keys, all_values))
    mixed_rows = mixed_seqs.reshape(row_count, HQ * HD)
    middle = x_rows + jnp.dot(mixed_rows, wo_all, preferred_element_type=f32)
    inverse_two = lax.rsqrt(jnp.mean(middle * middle, axis=-1, keepdims=True) + EPS)
    second_in = (middle * inverse_two * gain_second.astype(f32)).astype(bf16)
    gate_up = jnp.dot(second_in, gu_all, preferred_element_type=f32)
    hidden_width = gate_up.shape[1] // 2
    gate_proj, up_proj = gate_up[:, :hidden_width], gate_up[:, hidden_width:]
    hidden = (jax.nn.silu(gate_proj) * up_proj).astype(bf16)
    out_rows = middle + jnp.dot(hidden, wd_all, preferred_element_type=f32)
    result = out_rows.astype(bf16).reshape(hidden_in.shape)
    grad_rows = cotangent.reshape(row_count, width).astype(f32)
    grad_branch = grad_rows.astype(bf16)
    dw_down = jnp.einsum("rd,rf->df", grad_branch, hidden, preferred_element_type=f32)
    grad_hidden = jnp.einsum("rd,fd->rf", grad_branch, wd_all, preferred_element_type=f32)
    sigmoid_gate = jax.nn.sigmoid(gate_proj)
    grad_gate_proj = (
        grad_hidden * up_proj * sigmoid_gate * (1.0 + gate_proj * (1.0 - sigmoid_gate))
    ).astype(bf16)
    grad_up_proj = (grad_hidden * gate_proj * sigmoid_gate).astype(bf16)
    grad_gu = jnp.concatenate([grad_gate_proj, grad_up_proj], axis=1)
    dw_gu = jnp.einsum("rd,rf->df", second_in, grad_gu, preferred_element_type=f32)
    grad_second = jnp.einsum("rf,df->rd", grad_gu, gu_all, preferred_element_type=f32)
    grad_norm_two, dg_second = norm_back(
        middle, inverse_two, gain_second.astype(f32), grad_second
    )
    grad_middle = grad_rows + grad_norm_two
    grad_attn = grad_middle.astype(bf16)
    dw_out = jnp.einsum("rf,rd->fd", mixed_rows, grad_attn, preferred_element_type=f32)
    grad_mixed = jnp.einsum("rd,fd->rf", grad_attn, wo_all, preferred_element_type=f32).astype(
        bf16
    )
    grad_mixed_seqs = grad_mixed.reshape(seq_count, pair_rows, HK, group_size, HD)
    def backward_group(parts):
        query_grp, key_grp, value_grp, grad_grp, log_grp = parts
        scores = (
            jnp.einsum("qrd,kd->rqk", query_grp, key_grp, preferred_element_type=f32) * score_scale
        )
        scores = jnp.where(allowed, scores, -1e30)
        probs = jnp.exp(scores - log_grp[..., None])
        grad_probs = jnp.einsum("qrd,kd->rqk", grad_grp, value_grp, preferred_element_type=f32)
        row_dot = jnp.sum(grad_probs * probs, axis=-1, keepdims=True)
        grad_scores = (probs * (grad_probs - row_dot)).astype(bf16)
        grad_query_grp = (
            jnp.einsum("rqk,kd->qrd", grad_scores, key_grp, preferred_element_type=f32)
            * score_scale
        )
        grad_key_grp = (
            jnp.einsum("rqk,qrd->kd", grad_scores, query_grp, preferred_element_type=f32)
            * score_scale
        )
        grad_value_grp = jnp.einsum(
            "rqk,qrd->kd", probs.astype(bf16), grad_grp, preferred_element_type=f32
        )
        return (grad_query_grp, grad_key_grp, grad_value_grp)

    def backward_seq(inputs):
        query_blk, key_blk, value_blk, grad_blk, log_blk = inputs
        key_full = jnp.moveaxis(key_blk.reshape(full_len, HK, HD), 1, 0)
        value_full = jnp.moveaxis(value_blk.reshape(full_len, HK, HD), 1, 0)
        grad_query_all, grad_key_all, grad_value_all = lax.map(
            backward_group,
            (
                jnp.moveaxis(query_blk, 1, 0),
                key_full,
                value_full,
                jnp.moveaxis(grad_blk, 1, 0),
                log_blk,
            ),
        )
        return (
            jnp.moveaxis(grad_query_all, 0, 1).reshape(pair_rows, HQ * HD),
            jnp.moveaxis(grad_key_all, 0, 1).reshape(full_len, HK * HD),
            jnp.moveaxis(grad_value_all, 0, 1).reshape(full_len, HK * HD),
        )

    grad_query_seqs, grad_key_seqs, grad_value_seqs = lax.map(
        backward_seq, (query_seqs, all_keys, all_values, grad_mixed_seqs, log_sums)
    )
    dw_gu, dw_down, dw_out = (item.astype(bf16) for item in (dw_gu, dw_down, dw_out))
    piece = width // 4
    slab = dw_gu.shape[1] // 4
    down_cols = dw_down.shape[1] // 4
    pack_f = jnp.concatenate(
        [
            jnp.swapaxes(dw_gu.reshape(4, piece, 4, slab), 1, 2).reshape(4, 4 * piece, slab),
            dw_down.reshape(2, width // 2, 4, down_cols)
            .transpose(2, 1, 0, 3)
            .reshape(4, width // 2, slab),
            jnp.pad(dw_out.reshape(4, piece, width), ((0, 0), (0, 0), (0, slab - width))),
            jnp.pad(
                dg_second.astype(bf16).reshape(4, 1, piece), ((0, 0), (0, 0), (0, slab - piece))
            ),
        ],
        axis=1,
    )
    used_f = pack_f.shape[1]
    unit = 16 * ctx_count
    pack_f = jnp.pad(pack_f, ((0, 0), (0, -used_f % unit), (0, 0)))
    dkv = jnp.concatenate([grad_key_seqs, grad_value_seqs], axis=-1).astype(bf16)
    dkv = jnp.swapaxes(
        dkv.reshape(seq_count, ctx_count, pair_rows, 2 * k_width), 0, 1
    ).reshape(ctx_count, row_count, 2 * k_width)
    own_kv, part_f = kv_back(ctx_count, dkv, pack_f, 2)
    own_key_grad, own_value_grad = own_kv[:, :k_width], own_kv[:, k_width:]
    grad_query_lin = (
        rotate(grad_query_seqs.reshape(row_count, HQ, HD), cosine, -sine)
        .reshape(row_count, HQ * HD)
        .astype(bf16)
    )
    grad_key_lin = (
        rotate(own_key_grad.reshape(row_count, HK, HD), cosine, -sine)
        .reshape(row_count, HK * HD)
        .astype(bf16)
    )
    grad_value_lin = own_value_grad.reshape(row_count, HK * HD).astype(bf16)
    grad_lin = jnp.concatenate([grad_query_lin, grad_key_lin, grad_value_lin], axis=1)
    dw_qkv = jnp.einsum("rd,rf->df", first_in, grad_lin, preferred_element_type=f32)
    grad_first = jnp.einsum("rf,df->rd", grad_lin, qkv_all, preferred_element_type=f32)
    grad_norm_one, dg_first = norm_back(x_rows, inverse_one, gain_first.astype(f32), grad_first)
    grad_in_rows = grad_middle + grad_norm_one
    narrow = 256
    pack_q = jnp.pad(dw_qkv.astype(bf16), ((0, 0), (0, -dw_qkv.shape[1] % narrow)))
    strips = pack_q.shape[1] // narrow
    pack_q = jnp.swapaxes(pack_q.reshape(4, piece, strips, narrow), 1, 2)
    pack_q = jnp.concatenate(
        [
            pack_q.reshape(4, strips * piece, narrow),
            jnp.pad(
                dg_first.astype(bf16).reshape(4, 1, piece), ((0, 0), (0, 0), (0, narrow - piece))
            ),
        ],
        axis=1,
    )
    pack_q = jnp.pad(pack_q, ((0, 0), (0, -pack_q.shape[1] % unit), (0, 0)))
    total_f, total_q = last_sum(ctx_count, part_f, pack_q, 3)
    total_f, total_q = total_f.astype(f32), total_q.astype(f32)
    out_gu = jnp.swapaxes(total_f[: 4 * piece].reshape(4, piece, slab), 0, 1).reshape(piece, -1)
    at = 4 * piece
    out_down = total_f[at : at + width // 2].reshape(width // 2, 2, down_cols)
    out_down = jnp.swapaxes(out_down, 0, 1).reshape(width, down_cols).T
    at += width // 2
    out_wo = total_f[at : at + piece, :width]
    out_g2 = total_f[at + piece, :piece]
    at = strips * piece
    out_qkv = jnp.swapaxes(total_q[:at].reshape(strips, piece, narrow), 0, 1).reshape(piece, -1)
    return (
        result,
        grad_in_rows.reshape(hidden_in.shape),
        out_qkv[:, :q_width],
        out_qkv[:, q_width : q_width + k_width],
        out_qkv[:, q_width + k_width : q_width + 2 * k_width],
        out_wo,
        out_gu[:, :hidden_width],
        out_gu[:, hidden_width:],
        out_down,
        total_q[at, :piece],
        out_g2,
    )


def solution(mesh):
    in_specs = (
        P("fsdp", "ctx", None, None),
        P("fsdp", "ctx", None, None),
        P(),
        P("fsdp", "ctx", None),
        P("fsdp"),
        P("fsdp", None),
        P("fsdp", None),
        P("fsdp", None),
        P("fsdp", None),
        P("fsdp"),
        P("fsdp", None),
        P("fsdp", None),
        P("fsdp", None),
    )
    out_specs = (
        P("fsdp", "ctx", None, None),
        P("fsdp", "ctx", None, None),
        P("fsdp", None),
        P("fsdp", None),
        P("fsdp", None),
        P("fsdp", None),
        P("fsdp", None),
        P("fsdp", None),
        P("fsdp", None),
        P("fsdp"),
        P("fsdp"),
    )
    return jax.shard_map(shards, mesh=mesh, in_specs=in_specs, out_specs=out_specs, check_vma=False)
```

```python
import functools
import math

import jax
import jax.numpy as jnp
from jax import lax
from jax.experimental import pallas as pl
from jax.experimental.pallas import tpu as pltpu
from jax.sharding import PartitionSpec as P

HQ = 9
HK = 3
HD = 64


EPS = 1e-05
THETA = 100000.0


def rotate(vector, cosine, sine):
    half_dim = vector.shape[-1] // 2
    first = vector[..., :half_dim]
    second = vector[..., half_dim:]
    return jnp.concatenate(
        [first * cosine - second * sine, second * cosine + first * sine], axis=-1
    )


def rope_tables(place, head_dim):
    half_dim = head_dim // 2
    inverse = jnp.exp(jnp.arange(half_dim, dtype=jnp.float32) * (-math.log(THETA) / half_dim))
    angles = place.astype(jnp.float32)[:, None] * inverse[None, :]
    return (jnp.cos(angles)[:, None, :], jnp.sin(angles)[:, None, :])


def norm_back(vector, inverse, gain_vec, incoming):
    scaled = incoming * gain_vec
    gain_grad = jnp.sum(incoming * vector * inverse, axis=0)
    vector_grad = inverse * scaled - vector * (inverse * inverse * inverse) * jnp.mean(
        scaled * vector, axis=-1, keepdims=True
    )
    return (vector_grad, gain_grad)


MESH = pl.DeviceIdType.MESH
VMEM = pltpu.VMEM
BIG = 56 * 1024 * 1024


def ring_pos(index, count):
    odd = lax.rem(index, 2)
    return (1 - odd) * (index // 2) + odd * (count - 1 - index // 2)


def ring_index(place, count):
    place = lax.rem(place + 2 * count, count)
    back = place // (count // 2)
    return (1 - back) * (2 * place) + back * (2 * (count - 1 - place) + 1)


def neighbours(count):
    me = lax.axis_index("ctx")
    shard = lax.axis_index("fsdp")
    place = ring_pos(me, count)
    core = shard + 1 - 2 * lax.rem(shard, 2)
    across = lax.rem(shard + 2, 4)
    right = (ring_index(place + 1, count), shard)
    left = (ring_index(place - 1, count), shard)
    return me, shard, place, (me, core), (me, across), right, left


def greet(partners):
    barrier = pltpu.get_barrier_semaphore()
    for partner in partners:
        pl.semaphore_signal(barrier, inc=1, device_id=partner, device_id_type=MESH)
    pl.semaphore_wait(barrier, len(partners))


def remote(source, target, send, recv, device):
    return pltpu.make_async_remote_copy(
        src_ref=source,
        dst_ref=target,
        send_sem=send,
        recv_sem=recv,
        device_id=device,
        device_id_type=MESH,
    )


def comm_call(kernel, out_shape, scratch, cid, args):
    vm = pl.BlockSpec(memory_space=VMEM)
    return pl.pallas_call(
        kernel,
        out_shape=out_shape,
        in_specs=[vm] * len(args),
        out_specs=[vm] * len(out_shape),
        scratch_shapes=scratch,
        compiler_params=pltpu.CompilerParams(
            collective_id=cid, has_side_effects=True, vmem_limit_bytes=BIG
        ),
    )(*args)


class WeightGather:
    def __init__(self, ins, outs, sems, base, shard, core, across):
        self.parts = []
        for k, (src, dst) in enumerate(zip(ins, outs)):
            rows = src.shape[0]

            def slot(owner, dst=dst, rows=rows):
                return dst.at[pl.ds(pl.multiple_of(owner * rows, 16), rows)]

            other_core = shard + 1 - 2 * lax.rem(shard, 2)
            over = lax.rem(shard + 2, 4)
            sem = lambda j, k=k: (sems.at[0, base + k, j], sems.at[1, base + k, j])
            cross = remote(src, slot(shard), *sem(0), across)
            near = remote(src, slot(shard), *sem(1), core)
            onward = remote(slot(over), slot(over), *sem(2), core)
            self.parts.append((cross, near, onward, src, dst, shard, rows))

    def start(self):
        for cross, near, *_ in self.parts:
            cross.start()
            near.start()
        for _, _, _, src, dst, shard, rows in self.parts:
            dst[pl.ds(pl.multiple_of(shard * rows, 16), rows)] = src[...]

    def forward(self):
        for cross, _, onward, *_ in self.parts:
            cross.wait_recv()
            onward.start()

    def finish(self):
        for cross, near, onward, *_ in self.parts:
            near.wait_recv()
            onward.wait_recv()
            cross.wait_send()
            near.wait_send()
            onward.wait_send()


def gather_small(count, *refs):
    k = (len(refs) - 1) // 2
    ins, outs, sems = refs[:k], refs[k : 2 * k], refs[-1]
    _, shard, _, core, across, _, _ = neighbours(count)
    greet((core, across))
    work = WeightGather(ins, outs, sems, 0, shard, core, across)
    work.start()
    work.forward()
    work.finish()


def gather_weights(count, arrays, cid):
    outs = [jax.ShapeDtypeStruct((4 * a.shape[0], a.shape[1]), a.dtype) for a in arrays]
    return comm_call(
        functools.partial(gather_small, count),
        outs,
        [pltpu.SemaphoreType.DMA((2, len(arrays), 3))],
        cid,
        arrays,
    )


def gather_both_kernel(count, kv_ref, *refs):
    k = (len(refs) - 3) // 2
    ins, all_ref, outs = refs[:k], refs[k], refs[k + 1 : 2 * k + 1]
    sems, ring = refs[-2:]
    me, shard, place, core, across, right, left = neighbours(count)
    greet((core, across, right, left))
    half = count // 2
    rows = kv_ref.shape[0]

    def step(t, way):
        block = ring_index(place - way * (t - 1), count)
        src = kv_ref if t == 1 else all_ref.at[block]
        dst = all_ref.at[block]
        if t == half:
            cut = pl.ds(0, rows // 2) if way > 0 else pl.ds(rows // 2, rows // 2)
            src, dst = src.at[cut], dst.at[cut]
        lane = 0 if way > 0 else 1
        return remote(
            src, dst, ring.at[0, lane, t - 1], ring.at[1, lane, t - 1], right if way > 0 else left
        )

    steps = [(step(t, 1), step(t, -1)) for t in range(1, half + 1)]
    steps[0][0].start()
    steps[0][1].start()
    work = WeightGather(ins, outs, sems, 0, shard, core, across)
    work.start()
    all_ref[me] = kv_ref[...]
    for t in range(1, half):
        for way in (0, 1):
            steps[t - 1][way].wait_recv()
            steps[t][way].start()
    work.forward()
    for way in (0, 1):
        steps[half - 1][way].wait_recv()
    for pair in steps:
        pair[0].wait_send()
        pair[1].wait_send()
    work.finish()


def gather_both(count, kv, arrays, cid):
    outs = [jax.ShapeDtypeStruct((count,) + kv.shape, kv.dtype)]
    outs += [jax.ShapeDtypeStruct((4 * a.shape[0], a.shape[1]), a.dtype) for a in arrays]
    return comm_call(
        functools.partial(gather_both_kernel, count),
        outs,
        [
            pltpu.SemaphoreType.DMA((2, len(arrays), 3)),
            pltpu.SemaphoreType.DMA((2, 2, count // 2)),
        ],
        cid,
        [kv] + list(arrays),
    )


def add_rows(rows, block, body):
    def one(i, carry):
        body(pl.ds(pl.multiple_of(i * block, 16), block))
        return carry

    lax.fori_loop(0, rows // block, one, 0)


class ShardSum:
    def __init__(self, pack, out, near_buf, far_buf, sems, chunks, shard, core, across):
        self.pack, self.out, self.near_buf, self.far_buf = pack, out, near_buf, far_buf
        self.size = pack.shape[1] // chunks
        self.chunks = chunks
        self.mine, self.side = lax.rem(shard, 2), shard // 2
        self.near, self.far = [], []
        for c in range(chunks):
            cut = pl.ds(c * self.size, self.size)
            pair = []
            for x in range(2):
                pair.append(
                    remote(
                        pack.at[2 * x + 1 - self.mine, cut],
                        near_buf.at[x, cut],
                        sems.at[0, c, x],
                        sems.at[1, c, x],
                        core,
                    )
                )
            self.near.append(pair)
            self.far.append(
                remote(
                    near_buf.at[1 - self.side, cut],
                    far_buf.at[cut],
                    sems.at[0, c, 2],
                    sems.at[1, c, 2],
                    across,
                )
            )

    def start(self):
        for pair in self.near:
            for copy in pair:
                copy.start()

    def cross(self, c):
        for copy in self.near[c]:
            copy.wait_recv()

        def body(cut):
            for x in (0, 1):
                total = self.pack[2 * x + self.mine, cut].astype(jnp.float32) + self.near_buf[
                    x, cut
                ].astype(jnp.float32)
                self.near_buf[x, cut] = total.astype(jnp.bfloat16)

        base = c * self.size
        add_rows(self.size, 16, lambda cut: body(pl.ds(pl.multiple_of(base + cut.start, 16), cut.size)))
        self.far[c].start()

    def close(self, c):
        self.far[c].wait_recv()
        self.far[c].wait_send()

        def body(cut):
            total = self.near_buf[self.side, cut].astype(jnp.float32) + self.far_buf[cut].astype(
                jnp.float32
            )
            self.out[cut] = total.astype(jnp.bfloat16)

        base = c * self.size
        add_rows(self.size, 16, lambda cut: body(pl.ds(pl.multiple_of(base + cut.start, 16), cut.size)))

    def finish(self):
        for pair in self.near:
            for copy in pair:
                copy.wait_send()


class RingSum:
    def __init__(self, count, term, rows, cuts, send_buf, recv_buf, sems, place, right, left):
        self.count, self.term, self.rows, self.cuts = count, term, rows, cuts
        self.send_buf, self.recv_buf, self.place = send_buf, recv_buf, place
        self.half = count // 2
        self.copies = []
        for t in range(self.half):
            pair = []
            for lane in (0, 1):
                src, dst = send_buf.at[lane, t], recv_buf.at[lane, t]
                if t == 0:
                    src, dst = src.at[cuts[lane]], dst.at[cuts[lane]]
                pair.append(
                    remote(
                        src, dst, sems.at[0, lane, t], sems.at[1, lane, t], left if lane else right
                    )
                )
            self.copies.append(pair)

    def piece(self, t, lane):
        away = self.half - t
        return ring_index(self.place + (away if lane == 0 else -away), self.count)

    def start(self):
        for lane in (0, 1):
            index = self.piece(0, lane)
            cut = self.cuts[lane]
            self.send_buf[(lane, 0) + cut] = self.term(index)[cut]
            self.copies[0][lane].start()

    def step(self, t):
        for lane in (0, 1):
            self.copies[t - 1][lane].wait_recv()
            index = self.piece(t, lane)
            own = self.term(index)
            if t == 1:
                cut, rest = self.cuts[lane], self.cuts[1 - lane]
                self.send_buf[(lane, t) + rest] = own[rest]
                total = own[cut].astype(jnp.float32) + self.recv_buf[(lane, 0) + cut].astype(
                    jnp.float32
                )
                self.send_buf[(lane, t) + cut] = total.astype(jnp.bfloat16)
            else:

                def body(cut):
                    total = own[cut].astype(jnp.float32) + self.recv_buf[lane, t - 1, cut].astype(
                        jnp.float32
                    )
                    self.send_buf[lane, t, cut] = total.astype(jnp.bfloat16)

                add_rows(self.rows, 16, body)
            self.copies[t][lane].start()

    def last(self, store):
        for lane in (0, 1):
            self.copies[self.half - 1][lane].wait_recv()
        own = self.term(ring_index(self.place, self.count))

        def body(cut):
            total = (
                own[cut].astype(jnp.float32)
                + self.recv_buf[0, self.half - 1, cut].astype(jnp.float32)
                + self.recv_buf[1, self.half - 1, cut].astype(jnp.float32)
            )
            store(cut, total)

        add_rows(self.rows, 16, body)

    def finish(self):
        for pair in self.copies:
            for copy in pair:
                copy.wait_send()


def kv_back_kernel(
    count, chunks, dkv, pack, own_ref, sum_ref, near_buf, far_buf, sends, recvs, sems, ring
):
    me, shard, place, core, across, right, left = neighbours(count)
    greet((core, across, right, left))
    half = count // 2
    rows = dkv.shape[1]
    cuts = ((pl.ds(0, rows // 2),), (pl.ds(rows // 2, rows // 2),))
    turn = RingSum(count, lambda i: dkv.at[i], rows, cuts, sends, recvs, ring, place, right, left)
    turn.start()
    shares = ShardSum(pack, sum_ref, near_buf, far_buf, sems, chunks, shard, core, across)
    shares.start()
    for c in range(chunks):
        shares.cross(c)
    for t in range(1, half):
        turn.step(t)

    def store(cut, total):
        own_ref[cut] = total

    for c in range(chunks):
        shares.close(c)
    turn.last(store)
    turn.finish()
    shares.finish()


def kv_back(count, dkv, pack, cid):
    _, rows, width = dkv.shape
    _, prow, pwid = pack.shape
    chunks = 4
    bf16 = jnp.bfloat16
    half = count // 2
    return comm_call(
        functools.partial(kv_back_kernel, count, chunks),
        [
            jax.ShapeDtypeStruct((rows, width), jnp.float32),
            jax.ShapeDtypeStruct((prow, pwid), bf16),
        ],
        [
            VMEM((2, prow, pwid), bf16),
            VMEM((prow, pwid), bf16),
            VMEM((2, half, rows, width), bf16),
            VMEM((2, half, rows, width), bf16),
            pltpu.SemaphoreType.DMA((2, chunks, 3)),
            pltpu.SemaphoreType.DMA((2, 2, half)),
        ],
        cid,
        [dkv, pack],
    )


class RingGather:
    def __init__(self, count, out, rows, cuts, sems, place, right, left):
        half = count // 2
        self.copies = []
        for t in range(half):
            pair = []
            for lane in (0, 1):
                index = ring_index(place - t if lane == 0 else place + t, count)
                cut = (pl.ds(pl.multiple_of(index * rows, 16), rows),)
                if t == half - 1:
                    cut += cuts[lane][1:]
                pair.append(
                    remote(
                        out.at[cut],
                        out.at[cut],
                        sems.at[0, lane, t],
                        sems.at[1, lane, t],
                        left if lane else right,
                    )
                )
            self.copies.append(pair)

    def start(self):
        for copy in self.copies[0]:
            copy.start()

    def step(self, t):
        for lane in (0, 1):
            self.copies[t - 1][lane].wait_recv()
            self.copies[t][lane].start()

    def finish(self):
        for copy in self.copies[-1]:
            copy.wait_recv()
        for pair in self.copies:
            for copy in pair:
                copy.wait_send()


def ring_parts(count, source, out, sends, recvs, sems_sum, sems_all, place, right, left):
    rows, width = source.shape[0] // count, source.shape[1]
    cuts = ((slice(None), pl.ds(0, width // 2)), (slice(None), pl.ds(width // 2, width // 2)))
    term = lambda i: source.at[pl.ds(pl.multiple_of(i * rows, 16), rows)]
    turn = RingSum(count, term, rows, cuts, sends, recvs, sems_sum, place, right, left)
    spread = RingGather(count, out, rows, cuts, sems_all, place, right, left)
    base = ring_index(place, count) * rows

    def store(cut, total):
        out[pl.ds(pl.multiple_of(base + cut.start, 16), cut.size)] = total.astype(jnp.bfloat16)

    return turn, spread, store


def last_sum_kernel(
    count, part, pack, out_f, out_q, near_buf, far_buf, sum_q,
    sf, rf, sq, rq, sems, ra, rb, rc, rd,
):
    me, shard, place, core, across, right, left = neighbours(count)
    greet((core, across, right, left))
    half = count // 2
    shares = ShardSum(pack, sum_q, near_buf, far_buf, sems, 1, shard, core, across)
    shares.start()
    turn_f, spread_f, store_f = ring_parts(
        count, part, out_f, sf, rf, ra, rb, place, right, left
    )
    turn_q, spread_q, store_q = ring_parts(
        count, sum_q, out_q, sq, rq, rc, rd, place, right, left
    )
    turn_f.start()
    shares.cross(0)
    if half > 1:
        turn_f.step(1)
    shares.close(0)
    turn_q.start()
    for t in range(2, half + 1):
        if t < half:
            turn_f.step(t)
        turn_q.step(t - 1)
    turn_f.last(store_f)
    spread_f.start()
    turn_q.last(store_q)
    spread_q.start()
    for t in range(1, half):
        spread_f.step(t)
        spread_q.step(t)
    spread_f.finish()
    spread_q.finish()
    turn_f.finish()
    turn_q.finish()
    shares.finish()


def last_sum(count, part, pack, cid):
    frow, fwid = part.shape
    _, qrow, qwid = pack.shape
    bf16 = jnp.bfloat16
    half = count // 2
    dma = pltpu.SemaphoreType.DMA
    return comm_call(
        functools.partial(last_sum_kernel, count),
        [jax.ShapeDtypeStruct((frow, fwid), bf16), jax.ShapeDtypeStruct((qrow, qwid), bf16)],
        [
            VMEM((2, qrow, qwid), bf16),
            VMEM((qrow, qwid), bf16),
            VMEM((qrow, qwid), bf16),
            VMEM((2, half, frow // count, fwid), bf16),
            VMEM((2, half, frow // count, fwid), bf16),
            VMEM((2, half, qrow // count, qwid), bf16),
            VMEM((2, half, qrow // count, qwid), bf16),
            dma((2, 1, 3)),
            dma((2, 2, half)),
            dma((2, 2, half)),
            dma((2, 2, half)),
            dma((2, 2, half)),
        ],
        cid,
        [part, pack],
    )


def dot_t(left, right):
    return lax.dot_general(left, right, (((1,), (1,)), ((), ())), preferred_element_type=jnp.float32)


def head_stack(ref, rows, group, size):
    return jnp.concatenate(
        [ref[rows, (group * size + j) * HD : (group * size + j + 1) * HD] for j in range(size)],
        axis=0,
    )


def key_block(kv_ref, rows, first):
    block = kv_ref[:, rows, first : first + HD]
    return block.reshape(block.shape[0] * block.shape[1], HD)


def with_bias(scores, bias, size):
    span = bias.shape[0]
    return (scores.reshape(size, span, -1) + bias[None]).reshape(scores.shape)


def attend_kernel(pair, q_ref, kv_ref, bias_ref, o_ref, lse_ref):
    size = HQ // HK
    span = pair // 2
    f32 = jnp.float32
    bf16 = jnp.bfloat16

    def sequence(s, carry):
        low = pl.ds(pl.multiple_of(s * pair, 16), span)
        high = pl.ds(pl.multiple_of(s * pair + span, 16), span)
        for g in range(HK):
            keys = [key_block(kv_ref, rows, g * HD) for rows in (low, high)]
            values = [key_block(kv_ref, rows, (HK + g) * HD) for rows in (low, high)]
            for part, rows in enumerate((low, high)):
                query = head_stack(q_ref, rows, g, size)
                blocks = [dot_t(query, keys[j]) for j in range(part + 1)]
                blocks[part] = with_bias(blocks[part], bias_ref[part], size)
                top = jnp.max(blocks[0], axis=-1, keepdims=True)
                if part:
                    top = jnp.maximum(top, jnp.max(blocks[1], axis=-1, keepdims=True))
                total, out = 0.0, 0.0
                for j, block in enumerate(blocks):
                    raised = jnp.exp(block - top)
                    total = total + jnp.sum(raised, axis=-1, keepdims=True)
                    out = out + jnp.dot(
                        raised.astype(bf16), values[j], preferred_element_type=f32
                    )
                out = (out / total).astype(bf16)
                lse = top + jnp.log(total)
                for j in range(size):
                    h = g * size + j
                    o_ref[rows, h * HD : (h + 1) * HD] = out[j * span : (j + 1) * span]
                    lse_ref[rows, h : h + 1] = lse[j * span : (j + 1) * span]
        return carry

    lax.fori_loop(0, q_ref.shape[0] // pair, sequence, 0)


def attend_back_kernel(pair, q_ref, kv_ref, bias_ref, o_ref, do_ref, lse_ref, dq_ref, dkv_ref):
    size = HQ // HK
    span = pair // 2
    count = kv_ref.shape[0]
    f32 = jnp.float32
    bf16 = jnp.bfloat16
    scale = 1.0 / math.sqrt(HD)

    def sequence(s, carry):
        low = pl.ds(pl.multiple_of(s * pair, 16), span)
        high = pl.ds(pl.multiple_of(s * pair + span, 16), span)
        for g in range(HK):
            keys = [key_block(kv_ref, rows, g * HD) for rows in (low, high)]
            values = [key_block(kv_ref, rows, (HK + g) * HD) for rows in (low, high)]
            key_grads, value_grads = [0.0, 0.0], [0.0, 0.0]
            for part, rows in enumerate((low, high)):
                query = head_stack(q_ref, rows, g, size)
                grad = head_stack(do_ref, rows, g, size)
                out = head_stack(o_ref, rows, g, size)
                lse = jnp.concatenate(
                    [lse_ref[rows, g * size + j : g * size + j + 1] for j in range(size)], axis=0
                )
                inner = jnp.sum(grad.astype(f32) * out.astype(f32), axis=-1, keepdims=True)
                query_t = query.astype(f32).T.astype(bf16)
                grad_t = grad.astype(f32).T.astype(bf16)
                dq = 0.0
                for j in range(part + 1):
                    scores = dot_t(query, keys[j])
                    if j == part:
                        scores = with_bias(scores, bias_ref[part], size)
                    probs = jnp.exp(scores - lse)
                    ds = (probs * (dot_t(grad, values[j]) - inner)).astype(bf16)
                    dq = dq + jnp.dot(ds, keys[j], preferred_element_type=f32)
                    key_grads[j] = key_grads[j] + jnp.dot(query_t, ds, preferred_element_type=f32)
                    value_grads[j] = value_grads[j] + jnp.dot(
                        grad_t, probs.astype(bf16), preferred_element_type=f32
                    )
                dq = dq * scale
                for j in range(size):
                    h = g * size + j
                    dq_ref[rows, h * HD : (h + 1) * HD] = dq[j * span : (j + 1) * span]
            for j, rows in enumerate((low, high)):
                for first, item in ((g * HD, key_grads[j]), ((HK + g) * HD, value_grads[j])):
                    dkv_ref[:, rows, first : first + HD] = (
                        item.T.astype(bf16).reshape(count, span, HD)
                    )
        return carry

    lax.fori_loop(0, q_ref.shape[0] // pair, sequence, 0)


def plain_call(kernel, out_shape, args, flops):
    vm = pl.BlockSpec(memory_space=VMEM)
    return pl.pallas_call(
        kernel,
        out_shape=out_shape,
        in_specs=[vm] * len(args),
        out_specs=jax.tree.map(lambda _: vm, out_shape),
        compiler_params=pltpu.CompilerParams(vmem_limit_bytes=BIG),
        cost_estimate=pl.CostEstimate(flops=flops, bytes_accessed=8_000_000, transcendentals=0),
    )(*args)


def pack_kernel(second_t, gu_ref, branch_t, hidden_ref, mixed_t, ga_ref, gain_ref, out_ref):
    f32 = jnp.float32
    bf16 = jnp.bfloat16
    width = second_t.shape[0]
    piece = width // 4
    slab = out_ref.shape[2]
    cols = hidden_ref.shape[1] // 4
    deep = width // 2
    at = 4 * piece + deep
    for f in range(4):
        mine = pl.ds(f * piece, piece)
        for s in range(4):
            out_ref[f, s * piece : (s + 1) * piece] = jnp.dot(
                second_t[mine], gu_ref[:, s * slab : (s + 1) * slab], preferred_element_type=f32
            ).astype(bf16)
        for h in range(2):
            out_ref[f, 4 * piece : at, h * cols : (h + 1) * cols] = jnp.dot(
                branch_t[h * deep : (h + 1) * deep],
                hidden_ref[:, f * cols : (f + 1) * cols],
                preferred_element_type=f32,
            ).astype(bf16)
        out_ref[f, at : at + piece, :width] = jnp.dot(
            mixed_t[mine], ga_ref[...], preferred_element_type=f32
        ).astype(bf16)
        out_ref[f, at : at + piece, width:] = jnp.zeros((piece, slab - width), bf16)
        out_ref[f, at + piece :] = gain_ref[f]


def shards(
    hidden_in,
    cotangent,
    span_table,
    positions,
    attn_gain,
    w_query,
    w_key,
    w_value,
    w_out,
    ffn_gain,
    w_gate,
    w_up,
    w_down,
):
    seq_count = hidden_in.shape[0]
    pair_rows = hidden_in.shape[2]
    width = hidden_in.shape[3]
    span_rows = pair_rows // 2
    ctx_count = lax.axis_size("ctx")
    full_len = ctx_count * pair_rows
    row_count = seq_count * pair_rows
    score_scale = 1.0 / math.sqrt(HD)
    f32 = jnp.float32
    bf16 = jnp.bfloat16
    places = jnp.arange(span_rows, dtype=jnp.int32)
    own_span = span_table[lax.axis_index("ctx")]
    bias = []
    for ids, own in (
        (span_table, own_span),
        (2 * ctx_count - 1 - span_table, 2 * ctx_count - 1 - own_span),
    ):
        key_order = (ids[:, None] * span_rows + places[None, :]).reshape(-1)
        query_order = own * span_rows + places
        bias.append(jnp.where(key_order[None, :] <= query_order[:, None], 0.0, -1e30))
    bias = jnp.stack(bias).astype(f32)
    gains_own = jnp.concatenate(
        [attn_gain[None], ffn_gain[None], jnp.zeros((14,) + attn_gain.shape, bf16)], axis=0
    )
    qkv_all, gains_all = gather_weights(
        ctx_count, [jnp.concatenate([w_query, w_key, w_value], axis=1), gains_own], 0
    )
    gains_all = gains_all.reshape(4, 16, -1)
    gain_first = gains_all[:, 0].reshape(width)
    gain_second = gains_all[:, 1].reshape(width)
    cosine, sine = rope_tables(positions.reshape(row_count), HD)
    x_rows = hidden_in.reshape(row_count, width).astype(f32)
    inverse_one = lax.rsqrt(jnp.mean(x_rows * x_rows, axis=-1, keepdims=True) + EPS)
    first_in = (x_rows * inverse_one * gain_first.astype(f32)).astype(bf16)
    qkv_rows = jnp.dot(first_in, qkv_all, preferred_element_type=f32)
    q_width, k_width = HQ * HD, HK * HD
    query_rows = rotate(
        qkv_rows[:, :q_width].reshape(row_count, HQ, HD), cosine, sine
    ).astype(bf16)
    key_rows = rotate(
        qkv_rows[:, q_width : q_width + k_width].reshape(row_count, HK, HD), cosine, sine
    ).astype(bf16)
    value_rows = qkv_rows[:, q_width + k_width :].astype(bf16)
    all_kv, wo_all, gu_all, wd_all = gather_both(
        ctx_count,
        jnp.concatenate([key_rows.reshape(row_count, k_width), value_rows], axis=1),
        [w_out, jnp.concatenate([w_gate, w_up], axis=1), w_down],
        1,
    )
    query_rows = query_rows.reshape(row_count, q_width) * jnp.asarray(score_scale, bf16)
    flops = 4 * HQ * row_count * full_len * HD
    mixed_rows, log_sums = plain_call(
        functools.partial(attend_kernel, pair_rows),
        [
            jax.ShapeDtypeStruct((row_count, q_width), bf16),
            jax.ShapeDtypeStruct((row_count, 128), f32),
        ],
        [query_rows, all_kv, bias],
        flops,
    )
    middle = x_rows + jnp.dot(mixed_rows, wo_all, preferred_element_type=f32)
    inverse_two = lax.rsqrt(jnp.mean(middle * middle, axis=-1, keepdims=True) + EPS)
    second_in = (middle * inverse_two * gain_second.astype(f32)).astype(bf16)
    gate_up = jnp.dot(second_in, gu_all, preferred_element_type=f32)
    hidden_width = gate_up.shape[1] // 2
    gate_proj, up_proj = gate_up[:, :hidden_width], gate_up[:, hidden_width:]
    hidden = (jax.nn.silu(gate_proj) * up_proj).astype(bf16)
    out_rows = middle + jnp.dot(hidden, wd_all, preferred_element_type=f32)
    result = out_rows.astype(bf16).reshape(hidden_in.shape)
    grad_rows = cotangent.reshape(row_count, width).astype(f32)
    grad_branch = grad_rows.astype(bf16)
    grad_hidden = jnp.einsum("rd,fd->rf", grad_branch, wd_all, preferred_element_type=f32)
    sigmoid_gate = jax.nn.sigmoid(gate_proj)
    grad_gate_proj = (
        grad_hidden * up_proj * sigmoid_gate * (1.0 + gate_proj * (1.0 - sigmoid_gate))
    ).astype(bf16)
    grad_up_proj = (grad_hidden * gate_proj * sigmoid_gate).astype(bf16)
    grad_gu = jnp.concatenate([grad_gate_proj, grad_up_proj], axis=1)
    grad_second = jnp.einsum("rf,df->rd", grad_gu, gu_all, preferred_element_type=f32)
    grad_norm_two, dg_second = norm_back(
        middle, inverse_two, gain_second.astype(f32), grad_second
    )
    grad_middle = grad_rows + grad_norm_two
    grad_attn = grad_middle.astype(bf16)
    grad_mixed = jnp.einsum("rd,fd->rf", grad_attn, wo_all, preferred_element_type=f32).astype(
        bf16
    )
    piece = width // 4
    slab = grad_gu.shape[1] // 4
    down_cols = hidden_width // 4
    unit = 16 * ctx_count
    used_f = 5 * piece + width // 2
    rows_f = -(-(used_f + 1) // unit) * unit
    gain_rows = jnp.pad(
        dg_second.astype(bf16).reshape(4, 1, piece),
        ((0, 0), (0, rows_f - used_f - 1), (0, slab - piece)),
    )
    pack_f = plain_call(
        pack_kernel,
        jax.ShapeDtypeStruct((4, rows_f, slab), bf16),
        [second_in.T, grad_gu, grad_branch.T, hidden, mixed_rows.T, grad_attn, gain_rows],
        3 * flops,
    )
    grad_query_rows, dkv = plain_call(
        functools.partial(attend_back_kernel, pair_rows),
        [
            jax.ShapeDtypeStruct((row_count, q_width), f32),
            jax.ShapeDtypeStruct((ctx_count, row_count, 2 * k_width), bf16),
        ],
        [query_rows, all_kv, bias, mixed_rows, grad_mixed, log_sums],
        3 * flops,
    )
    own_kv, part_f = kv_back(ctx_count, dkv, pack_f, 2)
    own_key_grad, own_value_grad = own_kv[:, :k_width], own_kv[:, k_width:]
    grad_query_lin = (
        rotate(grad_query_rows.reshape(row_count, HQ, HD), cosine, -sine)
        .reshape(row_count, HQ * HD)
        .astype(bf16)
    )
    grad_key_lin = (
        rotate(own_key_grad.reshape(row_count, HK, HD), cosine, -sine)
        .reshape(row_count, HK * HD)
        .astype(bf16)
    )
    grad_value_lin = own_value_grad.reshape(row_count, HK * HD).astype(bf16)
    grad_lin = jnp.concatenate([grad_query_lin, grad_key_lin, grad_value_lin], axis=1)
    dw_qkv = jnp.einsum("rd,rf->df", first_in, grad_lin, preferred_element_type=f32)
    grad_first = jnp.einsum("rf,df->rd", grad_lin, qkv_all, preferred_element_type=f32)
    grad_norm_one, dg_first = norm_back(x_rows, inverse_one, gain_first.astype(f32), grad_first)
    grad_in_rows = grad_middle + grad_norm_one
    narrow = 256
    pack_q = jnp.pad(dw_qkv.astype(bf16), ((0, 0), (0, -dw_qkv.shape[1] % narrow)))
    strips = pack_q.shape[1] // narrow
    pack_q = jnp.swapaxes(pack_q.reshape(4, piece, strips, narrow), 1, 2)
    pack_q = jnp.concatenate(
        [
            pack_q.reshape(4, strips * piece, narrow),
            jnp.pad(
                dg_first.astype(bf16).reshape(4, 1, piece), ((0, 0), (0, 0), (0, narrow - piece))
            ),
        ],
        axis=1,
    )
    pack_q = jnp.pad(pack_q, ((0, 0), (0, -pack_q.shape[1] % unit), (0, 0)))
    total_f, total_q = last_sum(ctx_count, part_f, pack_q, 3)
    total_f, total_q = total_f.astype(f32), total_q.astype(f32)
    out_gu = jnp.swapaxes(total_f[: 4 * piece].reshape(4, piece, slab), 0, 1).reshape(piece, -1)
    at = 4 * piece
    out_down = total_f[at : at + width // 2].reshape(width // 2, 2, down_cols)
    out_down = jnp.swapaxes(out_down, 0, 1).reshape(width, down_cols).T
    at += width // 2
    out_wo = total_f[at : at + piece, :width]
    out_g2 = total_f[at + piece, :piece]
    at = strips * piece
    out_qkv = jnp.swapaxes(total_q[:at].reshape(strips, piece, narrow), 0, 1).reshape(piece, -1)
    return (
        result,
        grad_in_rows.reshape(hidden_in.shape),
        out_qkv[:, :q_width],
        out_qkv[:, q_width : q_width + k_width],
        out_qkv[:, q_width + k_width : q_width + 2 * k_width],
        out_wo,
        out_gu[:, :hidden_width],
        out_gu[:, hidden_width:],
        out_down,
        total_q[at, :piece],
        out_g2,
    )


def solution(mesh):
    in_specs = (
        P("fsdp", "ctx", None, None),
        P("fsdp", "ctx", None, None),
        P(),
        P("fsdp", "ctx", None),
        P("fsdp"),
        P("fsdp", None),
        P("fsdp", None),
        P("fsdp", None),
        P("fsdp", None),
        P("fsdp"),
        P("fsdp", None),
        P("fsdp", None),
        P("fsdp", None),
    )
    out_specs = (
        P("fsdp", "ctx", None, None),
        P("fsdp", "ctx", None, None),
        P("fsdp", None),
        P("fsdp", None),
        P("fsdp", None),
        P("fsdp", None),
        P("fsdp", None),
        P("fsdp", None),
        P("fsdp", None),
        P("fsdp"),
        P("fsdp"),
    )
    return jax.shard_map(shards, mesh=mesh, in_specs=in_specs, out_specs=out_specs, check_vma=False)
```

```python
import functools
import math

import jax
import jax.numpy as jnp
from jax import lax
from jax.experimental import pallas as pl
from jax.experimental.pallas import tpu as pltpu
from jax.sharding import PartitionSpec as P

HQ = 9
HK = 3
HD = 64


EPS = 1e-05
THETA = 100000.0


def rotate(vector, cosine, sine):
    half_dim = vector.shape[-1] // 2
    first = vector[..., :half_dim]
    second = vector[..., half_dim:]
    return jnp.concatenate(
        [first * cosine - second * sine, second * cosine + first * sine], axis=-1
    )


def rope_tables(place, head_dim):
    half_dim = head_dim // 2
    inverse = jnp.exp(jnp.arange(half_dim, dtype=jnp.float32) * (-math.log(THETA) / half_dim))
    angles = place.astype(jnp.float32)[:, None] * inverse[None, :]
    return (jnp.cos(angles)[:, None, :], jnp.sin(angles)[:, None, :])


def norm_back(vector, inverse, gain_vec, incoming):
    scaled = incoming * gain_vec
    gain_grad = jnp.sum(incoming * vector * inverse, axis=0)
    vector_grad = inverse * scaled - vector * (inverse * inverse * inverse) * jnp.mean(
        scaled * vector, axis=-1, keepdims=True
    )
    return (vector_grad, gain_grad)


MESH = pl.DeviceIdType.MESH
VMEM = pltpu.VMEM
BIG = 56 * 1024 * 1024


def ring_pos(index, count):
    odd = lax.rem(index, 2)
    return (1 - odd) * (index // 2) + odd * (count - 1 - index // 2)


def ring_index(place, count):
    place = lax.rem(place + 2 * count, count)
    back = place // (count // 2)
    return (1 - back) * (2 * place) + back * (2 * (count - 1 - place) + 1)


def neighbours(count):
    me = lax.axis_index("ctx")
    shard = lax.axis_index("fsdp")
    place = ring_pos(me, count)
    core = shard + 1 - 2 * lax.rem(shard, 2)
    across = lax.rem(shard + 2, 4)
    right = (ring_index(place + 1, count), shard)
    left = (ring_index(place - 1, count), shard)
    return me, shard, place, (me, core), (me, across), right, left


def greet(partners):
    barrier = pltpu.get_barrier_semaphore()
    for partner in partners:
        pl.semaphore_signal(barrier, inc=1, device_id=partner, device_id_type=MESH)
    pl.semaphore_wait(barrier, len(partners))


def remote(source, target, send, recv, device):
    return pltpu.make_async_remote_copy(
        src_ref=source,
        dst_ref=target,
        send_sem=send,
        recv_sem=recv,
        device_id=device,
        device_id_type=MESH,
    )


def comm_call(kernel, out_shape, scratch, cid, args):
    vm = pl.BlockSpec(memory_space=VMEM)
    return pl.pallas_call(
        kernel,
        out_shape=out_shape,
        in_specs=[vm] * len(args),
        out_specs=[vm] * len(out_shape),
        scratch_shapes=scratch,
        compiler_params=pltpu.CompilerParams(
            collective_id=cid, has_side_effects=True, vmem_limit_bytes=BIG
        ),
    )(*args)


class WeightGather:
    def __init__(self, ins, outs, sems, base, shard, core, across):
        self.parts = []
        for k, (src, dst) in enumerate(zip(ins, outs)):
            rows = src.shape[0]

            def slot(owner, dst=dst, rows=rows):
                return dst.at[pl.ds(pl.multiple_of(owner * rows, 16), rows)]

            other_core = shard + 1 - 2 * lax.rem(shard, 2)
            over = lax.rem(shard + 2, 4)
            sem = lambda j, k=k: (sems.at[0, base + k, j], sems.at[1, base + k, j])
            cross = remote(src, slot(shard), *sem(0), across)
            near = remote(src, slot(shard), *sem(1), core)
            onward = remote(slot(over), slot(over), *sem(2), core)
            self.parts.append((cross, near, onward, src, dst, shard, rows))

    def start(self):
        for cross, near, *_ in self.parts:
            cross.start()
            near.start()
        for _, _, _, src, dst, shard, rows in self.parts:
            dst[pl.ds(pl.multiple_of(shard * rows, 16), rows)] = src[...]

    def forward(self, k):
        cross, _, onward = self.parts[k][:3]
        cross.wait_recv()
        onward.start()

    def finish(self):
        for cross, near, onward, *_ in self.parts:
            near.wait_recv()
            onward.wait_recv()
            cross.wait_send()
            near.wait_send()
            onward.wait_send()


def gather_small(count, *refs):
    k = (len(refs) - 1) // 2
    ins, outs, sems = refs[:k], refs[k : 2 * k], refs[-1]
    _, shard, _, core, across, _, _ = neighbours(count)
    greet((core, across))
    work = WeightGather(ins, outs, sems, 0, shard, core, across)
    work.start()
    for j in range(k):
        work.forward(j)
    work.finish()


def gather_weights(count, arrays, cid):
    outs = [jax.ShapeDtypeStruct((4 * a.shape[0], a.shape[1]), a.dtype) for a in arrays]
    return comm_call(
        functools.partial(gather_small, count),
        outs,
        [pltpu.SemaphoreType.DMA((2, len(arrays), 3))],
        cid,
        arrays,
    )


def gather_both_kernel(count, kv_ref, *refs):
    k = (len(refs) - 3) // 2
    ins, all_ref, outs = refs[:k], refs[k], refs[k + 1 : 2 * k + 1]
    sems, ring = refs[-2:]
    me, shard, place, core, across, right, left = neighbours(count)
    greet((core, across, right, left))
    half = count // 2
    rows = kv_ref.shape[0]

    def step(t, way, sub):
        block = ring_index(place - way * (t - 1), count)
        src = kv_ref if t == 1 else all_ref.at[block]
        cut = pl.ds(sub * (rows // 2), rows // 2)
        lane = 0 if way > 0 else 1
        return remote(
            src.at[cut],
            all_ref.at[block, cut],
            ring.at[0, lane, t - 1, sub],
            ring.at[1, lane, t - 1, sub],
            right if way > 0 else left,
        )

    def group(t):
        if t == half:
            return [step(t, 1, 0), step(t, -1, 1)]
        return [step(t, 1, 0), step(t, -1, 1), step(t, 1, 1), step(t, -1, 0)]

    steps = [group(t) for t in range(1, half + 1)]
    for copy in steps[0]:
        copy.start()
    work = WeightGather(ins, outs, sems, 0, shard, core, across)
    work.start()
    all_ref[me] = kv_ref[...]
    sent = 0
    for t in range(1, half):
        if sent < k:
            work.forward(sent)
            sent += 1
        for j, copy in enumerate(steps[t - 1]):
            copy.wait_recv()
            if j < len(steps[t]):
                steps[t][j].start()
    while sent < k:
        work.forward(sent)
        sent += 1
    for copy in steps[half - 1]:
        copy.wait_recv()
    for pair in steps:
        for copy in pair:
            copy.wait_send()
    work.finish()


def gather_both(count, kv, arrays, cid):
    outs = [jax.ShapeDtypeStruct((count,) + kv.shape, kv.dtype)]
    outs += [jax.ShapeDtypeStruct((4 * a.shape[0], a.shape[1]), a.dtype) for a in arrays]
    return comm_call(
        functools.partial(gather_both_kernel, count),
        outs,
        [
            pltpu.SemaphoreType.DMA((2, len(arrays), 3)),
            pltpu.SemaphoreType.DMA((2, 2, count // 2, 2)),
        ],
        cid,
        [kv] + list(arrays),
    )


def add_rows(rows, width, body):
    block = max(b for b in range(16, 129, 16) if rows % b == 0 and b * width <= 64 * 768)

    def one(i, carry):
        body(pl.ds(pl.multiple_of(i * block, 16), block))
        return carry

    lax.fori_loop(0, rows // block, one, 0)


class ShardSum:
    def __init__(self, pack, out, near_buf, far_buf, sems, chunks, shard, core, across):
        self.pack, self.out, self.near_buf, self.far_buf = pack, out, near_buf, far_buf
        self.size = pack.shape[1] // chunks
        self.chunks, self.width = chunks, pack.shape[2]
        self.mine, self.side = lax.rem(shard, 2), shard // 2
        self.near, self.far = [], []
        for c in range(chunks):
            cut = pl.ds(c * self.size, self.size)
            pair = []
            for x in range(2):
                pair.append(
                    remote(
                        pack.at[2 * x + 1 - self.mine, cut],
                        near_buf.at[x, cut],
                        sems.at[0, c, x],
                        sems.at[1, c, x],
                        core,
                    )
                )
            self.near.append(pair)
            self.far.append(
                remote(
                    near_buf.at[1 - self.side, cut],
                    far_buf.at[cut],
                    sems.at[0, c, 2],
                    sems.at[1, c, 2],
                    across,
                )
            )

    def start(self):
        for pair in self.near:
            for copy in pair:
                copy.start()

    def cross(self, c):
        for copy in self.near[c]:
            copy.wait_recv()

        def body(cut):
            for x in (0, 1):
                total = self.pack[2 * x + self.mine, cut].astype(jnp.float32) + self.near_buf[
                    x, cut
                ].astype(jnp.float32)
                self.near_buf[x, cut] = total.astype(jnp.bfloat16)

        base = c * self.size
        add_rows(self.size, self.width, lambda cut: body(pl.ds(pl.multiple_of(base + cut.start, 16), cut.size)))
        self.far[c].start()

    def close(self, c):
        self.far[c].wait_recv()
        self.far[c].wait_send()

        def body(cut):
            total = self.near_buf[self.side, cut].astype(jnp.float32) + self.far_buf[cut].astype(
                jnp.float32
            )
            self.out[cut] = total.astype(jnp.bfloat16)

        base = c * self.size
        add_rows(self.size, self.width, lambda cut: body(pl.ds(pl.multiple_of(base + cut.start, 16), cut.size)))

    def finish(self):
        for pair in self.near:
            for copy in pair:
                copy.wait_send()


class RingSum:
    def __init__(self, count, term, rows, cuts, send_buf, recv_buf, sems, place, right, left):
        self.count, self.term, self.rows, self.cuts = count, term, rows, cuts
        self.send_buf, self.recv_buf, self.place = send_buf, recv_buf, place
        self.half, self.width = count // 2, send_buf.shape[3]
        self.copies = []
        for t in range(self.half):
            pair = []
            for lane in (0, 1):
                src, dst = send_buf.at[lane, t], recv_buf.at[lane, t]
                if t == 0:
                    src, dst = src.at[cuts[lane]], dst.at[cuts[lane]]
                pair.append(
                    remote(
                        src, dst, sems.at[0, lane, t], sems.at[1, lane, t], left if lane else right
                    )
                )
            self.copies.append(pair)

    def piece(self, t, lane):
        away = self.half - t
        return ring_index(self.place + (away if lane == 0 else -away), self.count)

    def start(self):
        for lane in (0, 1):
            index = self.piece(0, lane)
            cut = self.cuts[lane]
            self.send_buf[(lane, 0) + cut] = self.term(index)[cut]
            self.copies[0][lane].start()

    def step(self, t):
        for lane in (0, 1):
            self.copies[t - 1][lane].wait_recv()
            index = self.piece(t, lane)
            own = self.term(index)
            if t == 1:
                cut, rest = self.cuts[lane], self.cuts[1 - lane]
                self.send_buf[(lane, t) + rest] = own[rest]
                total = own[cut].astype(jnp.float32) + self.recv_buf[(lane, 0) + cut].astype(
                    jnp.float32
                )
                self.send_buf[(lane, t) + cut] = total.astype(jnp.bfloat16)
            else:

                def body(cut):
                    total = own[cut].astype(jnp.float32) + self.recv_buf[lane, t - 1, cut].astype(
                        jnp.float32
                    )
                    self.send_buf[lane, t, cut] = total.astype(jnp.bfloat16)

                add_rows(self.rows, self.width, body)
            self.copies[t][lane].start()

    def last(self, store):
        for lane in (0, 1):
            self.copies[self.half - 1][lane].wait_recv()
        own = self.term(ring_index(self.place, self.count))

        def body(cut):
            total = (
                own[cut].astype(jnp.float32)
                + self.recv_buf[0, self.half - 1, cut].astype(jnp.float32)
                + self.recv_buf[1, self.half - 1, cut].astype(jnp.float32)
            )
            store(cut, total)

        add_rows(self.rows, self.width, body)

    def finish(self):
        for pair in self.copies:
            for copy in pair:
                copy.wait_send()


def kv_back_kernel(
    count, chunks, dkv, pack, own_ref, sum_ref, near_buf, far_buf, sends, recvs, sems, ring
):
    me, shard, place, core, across, right, left = neighbours(count)
    greet((core, across, right, left))
    half = count // 2
    rows = dkv.shape[1]
    cuts = ((pl.ds(0, rows // 2),), (pl.ds(rows // 2, rows // 2),))
    turn = RingSum(count, lambda i: dkv.at[i], rows, cuts, sends, recvs, ring, place, right, left)
    turn.start()
    shares = ShardSum(pack, sum_ref, near_buf, far_buf, sems, chunks, shard, core, across)
    shares.start()
    shares.cross(0)
    for t in range(1, half):
        if t == half - 1:
            for c in range(chunks // 2):
                shares.close(c)
        turn.step(t)
        if t == 1:
            for c in range(1, chunks):
                shares.cross(c)

    def store(cut, total):
        own_ref[cut] = total

    for c in range(chunks // 2, chunks):
        shares.close(c)
    turn.last(store)
    turn.finish()
    shares.finish()


def kv_back(count, dkv, pack, cid):
    _, rows, width = dkv.shape
    _, prow, pwid = pack.shape
    chunks = 4
    bf16 = jnp.bfloat16
    half = count // 2
    return comm_call(
        functools.partial(kv_back_kernel, count, chunks),
        [
            jax.ShapeDtypeStruct((rows, width), jnp.float32),
            jax.ShapeDtypeStruct((prow, pwid), bf16),
        ],
        [
            VMEM((2, prow, pwid), bf16),
            VMEM((prow, pwid), bf16),
            VMEM((2, half, rows, width), bf16),
            VMEM((2, half, rows, width), bf16),
            pltpu.SemaphoreType.DMA((2, chunks, 3)),
            pltpu.SemaphoreType.DMA((2, 2, half)),
        ],
        cid,
        [dkv, pack],
    )


class RingGather:
    def __init__(self, count, out, rows, cuts, sems, place, right, left):
        half = count // 2
        self.copies = []
        for t in range(half):
            pair = []
            for lane in (0, 1):
                index = ring_index(place - t if lane == 0 else place + t, count)
                cut = (pl.ds(pl.multiple_of(index * rows, 16), rows),)
                if t == half - 1:
                    cut += cuts[lane][1:]
                pair.append(
                    remote(
                        out.at[cut],
                        out.at[cut],
                        sems.at[0, lane, t],
                        sems.at[1, lane, t],
                        left if lane else right,
                    )
                )
            self.copies.append(pair)

    def start(self):
        for copy in self.copies[0]:
            copy.start()

    def step(self, t):
        for lane in (0, 1):
            self.copies[t - 1][lane].wait_recv()
            self.copies[t][lane].start()

    def finish(self):
        for copy in self.copies[-1]:
            copy.wait_recv()
        for pair in self.copies:
            for copy in pair:
                copy.wait_send()


def ring_parts(count, source, out, sends, recvs, sems_sum, sems_all, place, right, left):
    rows, width = source.shape[0] // count, source.shape[1]
    cuts = ((slice(None), pl.ds(0, width // 2)), (slice(None), pl.ds(width // 2, width // 2)))
    term = lambda i: source.at[pl.ds(pl.multiple_of(i * rows, 16), rows)]
    turn = RingSum(count, term, rows, cuts, sends, recvs, sems_sum, place, right, left)
    spread = RingGather(count, out, rows, cuts, sems_all, place, right, left)
    base = ring_index(place, count) * rows

    def store(cut, total):
        out[pl.ds(pl.multiple_of(base + cut.start, 16), cut.size)] = total.astype(jnp.bfloat16)

    return turn, spread, store


def last_sum_kernel(
    count, part, pack, out_f, out_q, near_buf, far_buf, sum_q,
    sf, rf, sq, rq, sems, ra, rb, rc, rd,
):
    me, shard, place, core, across, right, left = neighbours(count)
    greet((core, across, right, left))
    half = count // 2
    shares = ShardSum(pack, sum_q, near_buf, far_buf, sems, 1, shard, core, across)
    shares.start()
    turn_f, spread_f, store_f = ring_parts(
        count, part, out_f, sf, rf, ra, rb, place, right, left
    )
    turn_q, spread_q, store_q = ring_parts(
        count, sum_q, out_q, sq, rq, rc, rd, place, right, left
    )
    turn_f.start()
    shares.cross(0)
    if half > 1:
        turn_f.step(1)
    shares.close(0)
    turn_q.start()
    for t in range(2, half + 1):
        if t < half:
            turn_f.step(t)
        turn_q.step(t - 1)
    turn_f.last(store_f)
    spread_f.start()
    turn_q.last(store_q)
    spread_q.start()
    for t in range(1, half):
        spread_f.step(t)
        spread_q.step(t)
    spread_f.finish()
    spread_q.finish()
    turn_f.finish()
    turn_q.finish()
    shares.finish()


def last_sum(count, part, pack, cid):
    frow, fwid = part.shape
    _, qrow, qwid = pack.shape
    bf16 = jnp.bfloat16
    half = count // 2
    dma = pltpu.SemaphoreType.DMA
    return comm_call(
        functools.partial(last_sum_kernel, count),
        [jax.ShapeDtypeStruct((frow, fwid), bf16), jax.ShapeDtypeStruct((qrow, qwid), bf16)],
        [
            VMEM((2, qrow, qwid), bf16),
            VMEM((qrow, qwid), bf16),
            VMEM((qrow, qwid), bf16),
            VMEM((2, half, frow // count, fwid), bf16),
            VMEM((2, half, frow // count, fwid), bf16),
            VMEM((2, half, qrow // count, qwid), bf16),
            VMEM((2, half, qrow // count, qwid), bf16),
            dma((2, 1, 3)),
            dma((2, 2, half)),
            dma((2, 2, half)),
            dma((2, 2, half)),
            dma((2, 2, half)),
        ],
        cid,
        [part, pack],
    )


def dot_t(left, right):
    return lax.dot_general(left, right, (((1,), (1,)), ((), ())), preferred_element_type=jnp.float32)


def head_stack(ref, rows, group, size):
    return jnp.concatenate(
        [ref[rows, (group * size + j) * HD : (group * size + j + 1) * HD] for j in range(size)],
        axis=0,
    )


def key_block(kv_ref, rows, first):
    block = kv_ref[:, rows, first : first + HD]
    return block.reshape(block.shape[0] * block.shape[1], HD)


def with_bias(scores, bias, size):
    span = bias.shape[0]
    return (scores.reshape(size, span, -1) + bias[None]).reshape(scores.shape)


def attend_kernel(pair, q_ref, kv_ref, bias_ref, o_ref, lse_ref):
    size = HQ // HK
    span = pair // 2
    f32 = jnp.float32
    bf16 = jnp.bfloat16

    def sequence(s, carry):
        low = pl.ds(pl.multiple_of(s * pair, 16), span)
        high = pl.ds(pl.multiple_of(s * pair + span, 16), span)
        for g in range(HK):
            keys = [key_block(kv_ref, rows, g * HD) for rows in (low, high)]
            values = [key_block(kv_ref, rows, (HK + g) * HD) for rows in (low, high)]
            for part, rows in enumerate((low, high)):
                query = head_stack(q_ref, rows, g, size)
                blocks = [dot_t(query, keys[j]) for j in range(part + 1)]
                blocks[part] = with_bias(blocks[part], bias_ref[part], size)
                top = jnp.max(blocks[0], axis=-1, keepdims=True)
                if part:
                    top = jnp.maximum(top, jnp.max(blocks[1], axis=-1, keepdims=True))
                total, out = 0.0, 0.0
                for j, block in enumerate(blocks):
                    raised = jnp.exp(block - top)
                    total = total + jnp.sum(raised, axis=-1, keepdims=True)
                    out = out + jnp.dot(
                        raised.astype(bf16), values[j], preferred_element_type=f32
                    )
                out = (out / total).astype(bf16)
                lse = top + jnp.log(total)
                for j in range(size):
                    h = g * size + j
                    o_ref[rows, h * HD : (h + 1) * HD] = out[j * span : (j + 1) * span]
                    lse_ref[rows, h : h + 1] = lse[j * span : (j + 1) * span]
        return carry

    lax.fori_loop(0, q_ref.shape[0] // pair, sequence, 0)


def attend_back_kernel(pair, q_ref, kv_ref, bias_ref, o_ref, do_ref, lse_ref, dq_ref, dkv_ref):
    size = HQ // HK
    span = pair // 2
    count = kv_ref.shape[0]
    f32 = jnp.float32
    bf16 = jnp.bfloat16
    scale = 1.0 / math.sqrt(HD)

    def sequence(s, carry):
        low = pl.ds(pl.multiple_of(s * pair, 16), span)
        high = pl.ds(pl.multiple_of(s * pair + span, 16), span)
        for g in range(HK):
            keys = [key_block(kv_ref, rows, g * HD) for rows in (low, high)]
            values = [key_block(kv_ref, rows, (HK + g) * HD) for rows in (low, high)]
            key_grads, value_grads = [0.0, 0.0], [0.0, 0.0]
            for part, rows in enumerate((low, high)):
                query = head_stack(q_ref, rows, g, size)
                grad = head_stack(do_ref, rows, g, size)
                out = head_stack(o_ref, rows, g, size)
                lse = jnp.concatenate(
                    [lse_ref[rows, g * size + j : g * size + j + 1] for j in range(size)], axis=0
                )
                inner = jnp.sum(grad.astype(f32) * out.astype(f32), axis=-1, keepdims=True)
                query_t = query.astype(f32).T.astype(bf16)
                grad_t = grad.astype(f32).T.astype(bf16)
                dq = 0.0
                for j in range(part + 1):
                    scores = dot_t(query, keys[j])
                    if j == part:
                        scores = with_bias(scores, bias_ref[part], size)
                    probs = jnp.exp(scores - lse)
                    ds = (probs * (dot_t(grad, values[j]) - inner)).astype(bf16)
                    dq = dq + jnp.dot(ds, keys[j], preferred_element_type=f32)
                    key_grads[j] = key_grads[j] + jnp.dot(query_t, ds, preferred_element_type=f32)
                    value_grads[j] = value_grads[j] + jnp.dot(
                        grad_t, probs.astype(bf16), preferred_element_type=f32
                    )
                dq = dq * scale
                for j in range(size):
                    h = g * size + j
                    dq_ref[rows, h * HD : (h + 1) * HD] = dq[j * span : (j + 1) * span]
            for j, rows in enumerate((low, high)):
                for first, item in ((g * HD, key_grads[j]), ((HK + g) * HD, value_grads[j])):
                    dkv_ref[:, rows, first : first + HD] = (
                        item.T.astype(bf16).reshape(count, span, HD)
                    )
        return carry

    lax.fori_loop(0, q_ref.shape[0] // pair, sequence, 0)


def plain_call(kernel, out_shape, args, flops):
    vm = pl.BlockSpec(memory_space=VMEM)
    return pl.pallas_call(
        kernel,
        out_shape=out_shape,
        in_specs=[vm] * len(args),
        out_specs=jax.tree.map(lambda _: vm, out_shape),
        compiler_params=pltpu.CompilerParams(vmem_limit_bytes=BIG),
        cost_estimate=pl.CostEstimate(flops=flops, bytes_accessed=8_000_000, transcendentals=0),
    )(*args)


def pack_kernel(second_t, gate_ref, up_ref, branch_t, hidden_ref, mixed_t, ga_ref, gain_ref, out_ref):
    f32 = jnp.float32
    bf16 = jnp.bfloat16
    width = second_t.shape[0]
    piece = width // 4
    slab = out_ref.shape[2]
    cols = hidden_ref.shape[1] // 4
    deep = width // 2
    at = 4 * piece + deep
    for f in range(4):
        mine = pl.ds(f * piece, piece)
        for s in range(4):
            out_ref[f, s * piece : (s + 1) * piece] = jnp.dot(
                second_t[mine],
                (gate_ref, up_ref)[s // 2][:, (s % 2) * slab : (s % 2 + 1) * slab],
                preferred_element_type=f32,
            ).astype(bf16)
        for h in range(2):
            out_ref[f, 4 * piece : at, h * cols : (h + 1) * cols] = jnp.dot(
                branch_t[h * deep : (h + 1) * deep],
                hidden_ref[:, f * cols : (f + 1) * cols],
                preferred_element_type=f32,
            ).astype(bf16)
        out_ref[f, at : at + piece, :width] = jnp.dot(
            mixed_t[mine], ga_ref[...], preferred_element_type=f32
        ).astype(bf16)
        out_ref[f, at : at + piece, width:] = jnp.zeros((piece, slab - width), bf16)
        out_ref[f, at + piece :] = gain_ref[f]


def unpack_kernel(f_ref, q_ref, *outs):
    f32 = jnp.float32
    query, key, value, out, gate, up, down, gain_one, gain_two = outs
    piece, width = query.shape
    slab, narrow = f_ref.shape[1], q_ref.shape[1]
    cols, deep = down.shape[0], width // 2
    for s in range(4):
        (gate, up)[s // 2][:, (s % 2) * slab : (s % 2 + 1) * slab] = f_ref[
            s * piece : (s + 1) * piece
        ].astype(f32)
    at = 4 * piece
    for h in range(2):
        block = f_ref[at : at + deep, h * cols : (h + 1) * cols].astype(f32)
        down[:, h * deep : (h + 1) * deep] = block.T
    at += deep
    out[...] = f_ref[at : at + piece, :width].astype(f32)
    gain_two[...] = f_ref[at + piece : at + piece + 16, :piece].astype(f32)[:1]
    total = width + 2 * key.shape[1]
    strips = -(-total // narrow)
    wide = jnp.concatenate(
        [q_ref[s * piece : (s + 1) * piece].astype(f32) for s in range(strips)], axis=1
    )
    query[...] = wide[:, :width]
    key[...] = wide[:, width : width + key.shape[1]]
    value[...] = wide[:, width + key.shape[1] : total]
    at = strips * piece
    gain_one[...] = q_ref[at : at + 16, :piece].astype(f32)[:1]


def shards(
    hidden_in,
    cotangent,
    span_table,
    positions,
    attn_gain,
    w_query,
    w_key,
    w_value,
    w_out,
    ffn_gain,
    w_gate,
    w_up,
    w_down,
):
    seq_count = hidden_in.shape[0]
    pair_rows = hidden_in.shape[2]
    width = hidden_in.shape[3]
    span_rows = pair_rows // 2
    ctx_count = lax.axis_size("ctx")
    full_len = ctx_count * pair_rows
    row_count = seq_count * pair_rows
    score_scale = 1.0 / math.sqrt(HD)
    f32 = jnp.float32
    bf16 = jnp.bfloat16
    places = jnp.arange(span_rows, dtype=jnp.int32)
    own_span = span_table[lax.axis_index("ctx")]
    bias = []
    for ids, own in (
        (span_table, own_span),
        (2 * ctx_count - 1 - span_table, 2 * ctx_count - 1 - own_span),
    ):
        key_order = (ids[:, None] * span_rows + places[None, :]).reshape(-1)
        query_order = own * span_rows + places
        bias.append(jnp.where(key_order[None, :] <= query_order[:, None], 0.0, -1e30))
    bias = jnp.stack(bias).astype(f32)
    gains_own = jnp.concatenate(
        [attn_gain[None], ffn_gain[None], jnp.zeros((14,) + attn_gain.shape, bf16)], axis=0
    )
    qkv_all, gains_all = gather_weights(
        ctx_count, [jnp.concatenate([w_query, w_key, w_value], axis=1), gains_own], 0
    )
    gains_all = gains_all.reshape(4, 16, -1)
    gain_first = gains_all[:, 0].reshape(width)
    gain_second = gains_all[:, 1].reshape(width)
    cosine, sine = rope_tables(positions.reshape(row_count), HD)
    x_rows = hidden_in.reshape(row_count, width).astype(f32)
    inverse_one = lax.rsqrt(jnp.mean(x_rows * x_rows, axis=-1, keepdims=True) + EPS)
    first_in = (x_rows * inverse_one * gain_first.astype(f32)).astype(bf16)
    qkv_rows = jnp.dot(first_in, qkv_all, preferred_element_type=f32)
    q_width, k_width = HQ * HD, HK * HD
    query_rows = rotate(
        qkv_rows[:, :q_width].reshape(row_count, HQ, HD), cosine, sine
    ).astype(bf16)
    key_rows = rotate(
        qkv_rows[:, q_width : q_width + k_width].reshape(row_count, HK, HD), cosine, sine
    ).astype(bf16)
    value_rows = qkv_rows[:, q_width + k_width :].astype(bf16)
    all_kv, wo_all, wg_all, wu_all, wd_all = gather_both(
        ctx_count,
        jnp.concatenate([key_rows.reshape(row_count, k_width), value_rows], axis=1),
        [w_out, w_gate, w_up, w_down],
        1,
    )
    query_rows = query_rows.reshape(row_count, q_width) * jnp.asarray(score_scale, bf16)
    flops = 4 * HQ * row_count * full_len * HD
    mixed_rows, log_sums = plain_call(
        functools.partial(attend_kernel, pair_rows),
        [
            jax.ShapeDtypeStruct((row_count, q_width), bf16),
            jax.ShapeDtypeStruct((row_count, 128), f32),
        ],
        [query_rows, all_kv, bias],
        flops,
    )
    middle = x_rows + jnp.dot(mixed_rows, wo_all, preferred_element_type=f32)
    inverse_two = lax.rsqrt(jnp.mean(middle * middle, axis=-1, keepdims=True) + EPS)
    second_in = (middle * inverse_two * gain_second.astype(f32)).astype(bf16)
    gate_proj = jnp.dot(second_in, wg_all, preferred_element_type=f32)
    up_proj = jnp.dot(second_in, wu_all, preferred_element_type=f32)
    hidden_width = gate_proj.shape[1]
    hidden = (jax.nn.silu(gate_proj) * up_proj).astype(bf16)
    out_rows = middle + jnp.dot(hidden, wd_all, preferred_element_type=f32)
    result = out_rows.astype(bf16).reshape(hidden_in.shape)
    grad_rows = cotangent.reshape(row_count, width).astype(f32)
    grad_branch = grad_rows.astype(bf16)
    grad_hidden = jnp.einsum("rd,fd->rf", grad_branch, wd_all, preferred_element_type=f32)
    sigmoid_gate = jax.nn.sigmoid(gate_proj)
    grad_gate_proj = (
        grad_hidden * up_proj * sigmoid_gate * (1.0 + gate_proj * (1.0 - sigmoid_gate))
    ).astype(bf16)
    grad_up_proj = (grad_hidden * gate_proj * sigmoid_gate).astype(bf16)
    grad_second = jnp.einsum(
        "rf,df->rd", grad_gate_proj, wg_all, preferred_element_type=f32
    ) + jnp.einsum("rf,df->rd", grad_up_proj, wu_all, preferred_element_type=f32)
    grad_norm_two, dg_second = norm_back(
        middle, inverse_two, gain_second.astype(f32), grad_second
    )
    grad_middle = grad_rows + grad_norm_two
    grad_attn = grad_middle.astype(bf16)
    grad_mixed = jnp.einsum("rd,fd->rf", grad_attn, wo_all, preferred_element_type=f32).astype(
        bf16
    )
    piece = width // 4
    slab = hidden_width // 2
    unit = 16 * ctx_count
    used_f = 5 * piece + width // 2
    rows_f = -(-(used_f + 1) // unit) * unit
    gain_rows = jnp.pad(
        dg_second.astype(bf16).reshape(4, 1, piece),
        ((0, 0), (0, rows_f - used_f - 1), (0, slab - piece)),
    )
    pack_f = plain_call(
        pack_kernel,
        jax.ShapeDtypeStruct((4, rows_f, slab), bf16),
        [second_in.T, grad_gate_proj, grad_up_proj, grad_branch.T, hidden, mixed_rows.T, grad_attn, gain_rows],
        3 * flops,
    )
    grad_query_rows, dkv = plain_call(
        functools.partial(attend_back_kernel, pair_rows),
        [
            jax.ShapeDtypeStruct((row_count, q_width), f32),
            jax.ShapeDtypeStruct((ctx_count, row_count, 2 * k_width), bf16),
        ],
        [query_rows, all_kv, bias, mixed_rows, grad_mixed, log_sums],
        3 * flops,
    )
    own_kv, part_f = kv_back(ctx_count, dkv, pack_f, 2)
    own_key_grad, own_value_grad = own_kv[:, :k_width], own_kv[:, k_width:]
    grad_query_lin = (
        rotate(grad_query_rows.reshape(row_count, HQ, HD), cosine, -sine)
        .reshape(row_count, HQ * HD)
        .astype(bf16)
    )
    grad_key_lin = (
        rotate(own_key_grad.reshape(row_count, HK, HD), cosine, -sine)
        .reshape(row_count, HK * HD)
        .astype(bf16)
    )
    grad_value_lin = own_value_grad.reshape(row_count, HK * HD).astype(bf16)
    grad_lin = jnp.concatenate([grad_query_lin, grad_key_lin, grad_value_lin], axis=1)
    dw_qkv = jnp.einsum("rd,rf->df", first_in, grad_lin, preferred_element_type=f32)
    grad_first = jnp.einsum("rf,df->rd", grad_lin, qkv_all, preferred_element_type=f32)
    grad_norm_one, dg_first = norm_back(x_rows, inverse_one, gain_first.astype(f32), grad_first)
    grad_in_rows = grad_middle + grad_norm_one
    narrow = 256
    pack_q = jnp.pad(dw_qkv.astype(bf16), ((0, 0), (0, -dw_qkv.shape[1] % narrow)))
    strips = pack_q.shape[1] // narrow
    pack_q = jnp.swapaxes(pack_q.reshape(4, piece, strips, narrow), 1, 2)
    pack_q = jnp.concatenate(
        [
            pack_q.reshape(4, strips * piece, narrow),
            jnp.pad(
                dg_first.astype(bf16).reshape(4, 1, piece), ((0, 0), (0, 0), (0, narrow - piece))
            ),
        ],
        axis=1,
    )
    pack_q = jnp.pad(pack_q, ((0, 0), (0, -pack_q.shape[1] % unit), (0, 0)))
    total_f, total_q = last_sum(ctx_count, part_f, pack_q, 3)
    shapes = [
        (piece, q_width),
        (piece, k_width),
        (piece, k_width),
        w_out.shape,
        w_gate.shape,
        w_up.shape,
        w_down.shape,
        (1, piece),
        (1, piece),
    ]
    grads = plain_call(
        unpack_kernel,
        [jax.ShapeDtypeStruct(shape, f32) for shape in shapes],
        [total_f, total_q],
        1_000_000,
    )
    return (
        result,
        grad_in_rows.reshape(hidden_in.shape),
        *grads[:7],
        grads[7].reshape(piece),
        grads[8].reshape(piece),
    )


def solution(mesh):
    in_specs = (
        P("fsdp", "ctx", None, None),
        P("fsdp", "ctx", None, None),
        P(),
        P("fsdp", "ctx", None),
        P("fsdp"),
        P("fsdp", None),
        P("fsdp", None),
        P("fsdp", None),
        P("fsdp", None),
        P("fsdp"),
        P("fsdp", None),
        P("fsdp", None),
        P("fsdp", None),
    )
    out_specs = (
        P("fsdp", "ctx", None, None),
        P("fsdp", "ctx", None, None),
        P("fsdp", None),
        P("fsdp", None),
        P("fsdp", None),
        P("fsdp", None),
        P("fsdp", None),
        P("fsdp", None),
        P("fsdp", None),
        P("fsdp"),
        P("fsdp"),
    )
    return jax.shard_map(shards, mesh=mesh, in_specs=in_specs, out_specs=out_specs, check_vma=False)
```
